32 devices in a mesh: frames: 4 (over y, x), height: 8 (over z, core).
Axes of the slice: x: 2, y: 2, z: 4, core: 2. Of those that a mesh axis runs over, the one named last changes fastest.
Arguments:
- latent: bfloat16 [4, 16, 160, 384], P('frames', 'height'), may hold values from -15 to 15
- first_gain: float32 [384], replicated, may hold values from 0.1 to 1.9
- first_shift: float32 [384], replicated, may hold values from -4 to 4
- query_weight: bfloat16 [384, 384], replicated
- key_weight: bfloat16 [384, 384], replicated
- value_weight: bfloat16 [384, 384], replicated, may hold values from -0.3125 to 0.3125
- out_weight: bfloat16 [384, 384], replicated, may hold values from -0.3125 to 0.3125
- out_bias: float32 [384], replicated, may hold values from -6 to 6
- second_gain: float32 [384], replicated, may hold values from 0.1 to 1.9
- second_shift: float32 [384], replicated, may hold values from -4 to 4
- up_weight: bfloat16 [3, 3, 3, 384, 384], replicated, may hold values from -0.15625 to 0.15625
- up_bias: float32 [384], replicated, may hold values from -6 to 6
Outputs:
- upsampled: bfloat16 [8, 32, 320, 384], P('frames', 'height')
The draws below stay inside these ranges and needn't reach their ends.
All inputs are finite; a program needn't handle non-finite values.
Results may differ from the reference program's by a relative error of at most 0.013.
Values may be sent and summed in bfloat16 or wider, within the bound.
No kernel may reach another device: no remote copies, remote signals or barrier semaphores. Data moves between devices by JAX's collectives and lax.ppermute only.
A program may use at most 128 MiB of HBM per device.

```python
import math
import jax
import jax.numpy as jnp
from jax import lax

C = 384
GROUPS = 32
WID = 160
ROWS_DEV = 2
F = 4
H = 16


def draw_latent(key, part):
    keys = jax.random.split(jax.random.fold_in(key, 11), 8)
    frame_pos = jnp.arange(F, dtype=jnp.float32)[:, None, None, None]
    row_index = jnp.arange(H, dtype=jnp.int32)
    row_pos = row_index.astype(jnp.float32)[None, :, None, None]
    ramp = 0.5 * (frame_pos / max(F - 1, 1) + row_pos / max(H - 1, 1))
    rough = jnp.exp(jax.random.uniform(keys[0], (F, H, WID, 1), jnp.float32, 0.0, math.log(3.3)))
    position_scale = jnp.exp(math.log(3.0) * ramp) * rough
    channel_scale = jnp.exp(jax.random.uniform(keys[1], (C,), jnp.float32, 0.0, math.log(10.0)))
    offsets = jax.random.normal(keys[2], (H // ROWS_DEV, C), jnp.float32)
    slab_offset = offsets[row_index // ROWS_DEV][None, :, None, :]
    frame_offset = 1.1 * jax.random.normal(keys[7], (F, 1, 1, C), jnp.float32)
    base = jax.random.normal(keys[3], (F, H, WID, C), jnp.float32)
    result = 0.3 * channel_scale * (position_scale * base + slab_offset + frame_offset)
    return (0.25 * jnp.clip(result, -60.0, 60.0)).astype(jnp.bfloat16)


def weight_pair(key):
    first_key, second_key = jax.random.split(jax.random.fold_in(key, 29))
    bound = 4.0 / math.sqrt(C)
    first = jax.random.normal(first_key, (C, C), jnp.float32) / math.sqrt(C)
    other = jax.random.normal(second_key, (C, C), jnp.float32) / math.sqrt(C)
    second = other
    return (jnp.clip(first, -bound, bound), jnp.clip(second, -bound, bound))


def draw_query_weight(key, part):
    return weight_pair(key)[0].astype(jnp.bfloat16)


def draw_key_weight(key, part):
    return weight_pair(key)[1].astype(jnp.bfloat16)


def normal_values(key, shape, scale, limit, held_as=jnp.bfloat16):
    drawn = scale * jax.random.normal(key, shape, jnp.float32)
    return jnp.clip(drawn, min=-limit, max=limit).astype(held_as)


def setup_inputs(seed: int = 0) -> dict:
    arg_keys = jax.random.split(jax.random.key(seed), 13)
    latent = draw_latent(jax.random.fold_in(arg_keys[12], 71), 0)
    first_gain = jnp.clip(1.0 + 0.18 * jax.random.normal(arg_keys[1], (C,), jnp.float32), 0.1, 1.9)
    first_shift = normal_values(arg_keys[2], (C,), 0.3, 4.0, jnp.float32)
    query_weight = draw_query_weight(jax.random.fold_in(arg_keys[12], 71), 0)
    key_weight = draw_key_weight(jax.random.fold_in(arg_keys[12], 71), 0)
    value_weight = normal_values(arg_keys[5], (C, C), C ** -0.5, 0.3125)
    out_weight = normal_values(arg_keys[6], (C, C), C ** -0.5, 0.3125)
    out_bias = normal_values(arg_keys[7], (C,), 0.5, 6.0, jnp.float32)
    second_gain = jnp.clip(1.0 + 0.18 * jax.random.normal(arg_keys[8], (C,), jnp.float32), 0.1, 1.9)
    second_shift = normal_values(arg_keys[9], (C,), 0.3, 4.0, jnp.float32)
    up_weight = normal_values(arg_keys[10], (3, 3, 3, C, C), (27 * C // 8) ** -0.5, 0.15625)
    up_bias = normal_values(arg_keys[11], (C,), 0.5, 6.0, jnp.float32)
    return dict(latent=latent, first_gain=first_gain, first_shift=first_shift, query_weight=query_weight, key_weight=key_weight, value_weight=value_weight, out_weight=out_weight, out_bias=out_bias, second_gain=second_gain, second_shift=second_shift, up_weight=up_weight, up_bias=up_bias)


EPS = 1e-05

def group_norm(value, gain, shift):
    floats = value.astype(jnp.float32)
    shape = floats.shape
    grouped = floats.reshape(shape[:-1] + (GROUPS, shape[-1] // GROUPS))
    mean = lax.optimization_barrier(jnp.mean(grouped, axis=(0, 1, 2, 4), keepdims=True))
    spread = lax.optimization_barrier(jnp.mean(jnp.square(grouped - mean), axis=(0, 1, 2, 4), keepdims=True))
    normal_part = ((grouped - mean) * lax.rsqrt(spread + EPS)).reshape(shape)
    return normal_part * gain + shift

def upsample_taps(current, earlier, weight, bias):
    rows = current.shape[0] - 1
    cols = current.shape[1] - 1
    width = current.shape[2]
    time_taps = (((0, current), (2, earlier)), ((1, current),))
    space_taps = (((1, 0),), ((2, 0), (0, 1)))
    frame_list = []
    for odd_time in range(2):
        row_list = []
        for odd_row in range(2):
            col_list = []
            for odd_col in range(2):
                summed = jnp.zeros((rows * cols, width), jnp.float32)
                for time_tap, source in time_taps[odd_time]:
                    for row_tap, row_step in space_taps[odd_row]:
                        for col_tap, col_step in space_taps[odd_col]:
                            window = source[row_step:row_step + rows, col_step:col_step + cols].reshape(-1, width)
                            summed = summed + jnp.dot(window, weight[time_tap, row_tap, col_tap], preferred_element_type=jnp.float32)
                col_list.append((summed + bias).reshape(rows, cols, width))
            row_list.append(jnp.stack(col_list, axis=2).reshape(rows, 2 * cols, width))
        frame_list.append(jnp.stack(row_list, axis=1).reshape(2 * rows, 2 * cols, width))
    return jnp.stack(frame_list, axis=0)

def reference(latent, first_gain, first_shift, query_weight, key_weight, value_weight, out_weight, out_bias, second_gain, second_shift, up_weight, up_bias):
    frames, rows, cols, width = latent.shape
    normed = group_norm(latent, first_gain, first_shift).astype(jnp.bfloat16)
    flat = normed.reshape(-1, width)
    queries = jnp.dot(flat, query_weight, preferred_element_type=jnp.float32).astype(jnp.bfloat16).reshape(frames, rows, cols, width)
    keys = jnp.dot(flat, key_weight, preferred_element_type=jnp.float32).astype(jnp.bfloat16).reshape(frames, rows * cols, width)
    values = jnp.dot(flat, value_weight, preferred_element_type=jnp.float32).astype(jnp.bfloat16).reshape(frames, rows * cols, width)
    factor = width ** (-0.5)

    def one_frame(inputs):
        frame_queries, frame_keys, frame_values = inputs

        def one_row(row_queries):
            scores = jnp.dot(row_queries, frame_keys.T, preferred_element_type=jnp.float32) * factor
            highest = lax.optimization_barrier(jnp.max(scores, axis=-1, keepdims=True))
            weights = jnp.exp(scores - highest)
            totals = lax.optimization_barrier(jnp.sum(weights, axis=-1, keepdims=True))
            summed = jnp.dot(weights.astype(jnp.bfloat16), frame_values, preferred_element_type=jnp.float32)
            return (summed / totals).astype(jnp.bfloat16)
        return lax.map(one_row, frame_queries)
    attended = lax.map(one_frame, (queries, keys, values))
    branch = jnp.dot(attended.reshape(-1, width), out_weight, preferred_element_type=jnp.float32).reshape(latent.shape) + out_bias
    mixed = (latent.astype(jnp.float32) + branch).astype(jnp.bfloat16)
    activated = jax.nn.silu(group_norm(mixed, second_gain, second_shift)).astype(jnp.bfloat16)
    padded = jnp.pad(activated, ((1, 0), (0, 1), (0, 1), (0, 0)))

    def one_output(index):
        current = lax.dynamic_index_in_dim(padded, index + 1, 0, keepdims=False)
        earlier = lax.dynamic_index_in_dim(padded, index, 0, keepdims=False)
        return upsample_taps(current, earlier, up_weight, up_bias).astype(jnp.bfloat16)
    result = lax.map(one_output, jnp.arange(frames, dtype=jnp.int32))
    return result.reshape(2 * frames, 2 * rows, 2 * cols, width)
```

```python
import functools
import math

import jax
import jax.numpy as jnp
import numpy as np
from jax import lax
from jax.experimental import pallas as pl
from jax.experimental.pallas import tpu as pltpu
from jax.sharding import PartitionSpec as P

GROUPS = 32
EPS = 1e-05
F32 = jnp.float32
BF16 = jnp.bfloat16
VMEM_LIMIT = 48 * 1024 * 1024


def swapped(value, axis, mask):
    count = lax.axis_size(axis)
    return lax.ppermute(value, axis, [(i, i ^ mask) for i in range(count)])


def group_matrix(width):
    group = np.arange(width) // (width // GROUPS)
    return jnp.asarray(group[:, None] == group[None, :], BF16)


def group_sum(vector, same_group):
    high = vector.astype(BF16).astype(F32)
    rest = vector - high
    middle = rest.astype(BF16).astype(F32)
    low = rest - middle
    row = lax.broadcasted_iota(jnp.int32, (8, vector.shape[1]), 0)
    parts = jnp.where(row == 0, high, jnp.where(row == 1, middle, jnp.where(row == 2, low, 0.0)))
    summed = jnp.dot(parts.astype(BF16), same_group, preferred_element_type=F32)
    return jnp.sum(summed, axis=0, keepdims=True)


def mean_and_spread(values, same_group):
    count = values.shape[0] * (values.shape[1] // GROUPS)
    mean = group_sum(jnp.sum(values, axis=0, keepdims=True), same_group) * (1.0 / count)
    centered = values - mean
    return mean, group_sum(jnp.sum(centered * centered, axis=0, keepdims=True), same_group)


def stats_kernel(x_ref, same_ref, out_ref):
    mean, spread = mean_and_spread(x_ref[...].astype(F32), same_ref[...])
    out_ref[0:1, :] = mean
    out_ref[1:2, :] = spread


def local_stats(block, same_group):
    positions, width = block.shape
    return pl.pallas_call(
        stats_kernel,
        out_shape=jax.ShapeDtypeStruct((2, width), F32),
        name="local_stats",
    )(block, same_group)


def merged(stats, other, count):
    gap = stats[0] - other[0]
    return jnp.stack(
        [0.5 * (stats[0] + other[0]), stats[1] + other[1] + gap * gap * (0.5 * count)]
    )


def attention_kernel(slabs, count, below_ref, stats_ref, gain_ref, shift_ref, qk_ref, vo_ref, bias_ref, same_ref, *refs):
    blocks = refs[:slabs]
    mixed_ref, out_stats_ref, keys, sems = refs[slabs:]
    positions, width = blocks[0].shape
    cols = positions // 2
    copies = [
        pltpu.make_async_copy(
            blocks[i], keys.at[pl.ds(i * positions, positions), :], sems.at[i]
        )
        for i in range(slabs)
    ]
    for copy in copies:
        copy.start()
    mean = stats_ref[0:1, :]
    factor = gain_ref[...] * lax.rsqrt(stats_ref[1:2, :] * (1.0 / count) + EPS)
    offset = shift_ref[...] - mean * factor
    scale = width ** (-0.5) * math.log2(math.e)
    for copy in copies:
        copy.wait()
    below = pl.multiple_of(below_ref[0] * positions, positions)
    for row in range(3):
        if row < 2:
            own = keys[row * cols : (row + 1) * cols, :].astype(F32)
        else:
            own = keys[pl.ds(below, cols), :].astype(F32)
        normed = ((own - mean) * factor + shift_ref[...]).astype(BF16)
        turned = jnp.dot(normed, qk_ref[...], preferred_element_type=F32) * scale
        constant = jnp.sum(turned * offset, axis=1, keepdims=True)
        queries = (turned * factor).astype(BF16)
        scores = lax.dot_general(
            queries, keys[...], (((1,), (1,)), ((), ())), preferred_element_type=F32
        )
        highest = jnp.max(scores, axis=1, keepdims=True) + constant
        probs = jnp.exp2(scores + (constant - highest)).astype(BF16)
        total = jnp.sum(probs.astype(F32), axis=1, keepdims=True)
        summed = jnp.dot(probs, keys[...], preferred_element_type=F32)
        attended = ((summed / total - mean) * factor + shift_ref[...]).astype(BF16)
        branch = jnp.dot(attended, vo_ref[...], preferred_element_type=F32) + bias_ref[...]
        mixed_ref[row * cols : (row + 1) * cols, :] = (own + branch).astype(BF16)
    mean, spread = mean_and_spread(mixed_ref[0:positions, :].astype(F32), same_ref[...])
    out_stats_ref[0:1, :] = mean
    out_stats_ref[1:2, :] = spread


def attention(blocks, below, stats, count, gain, shift, qk, vo, bias, same_group):
    slabs = len(blocks)
    positions, width = blocks[0].shape
    vmem = pl.BlockSpec(memory_space=pltpu.VMEM)
    return pl.pallas_call(
        functools.partial(attention_kernel, slabs, count),
        out_shape=(
            jax.ShapeDtypeStruct((positions // 2 * 3, width), BF16),
            jax.ShapeDtypeStruct((2, width), F32),
        ),
        in_specs=[pl.BlockSpec(memory_space=pltpu.SMEM)]
        + [vmem] * 7
        + [pl.BlockSpec(memory_space=pl.ANY)] * slabs,
        out_specs=(vmem, vmem),
        scratch_shapes=[
            pltpu.VMEM((slabs * positions, width), BF16),
            pltpu.SemaphoreType.DMA((slabs,)),
        ],
        compiler_params=pltpu.CompilerParams(vmem_limit_bytes=VMEM_LIMIT),
        name="attention",
    )(below, stats, gain, shift, qk, vo, bias, same_group, *blocks)


SPACE_TAPS = (((1, 0),), ((2, 0), (0, 1)))


def upsample_kernel(count, valid_ref, current_ref, earlier_ref, stats_ref, gain_ref, shift_ref, bias_ref, weight_hbm, out_hbm, active, weight, wide, out, weight_sems, out_sems):
    positions, width = current_ref.shape
    cols = positions // 3
    order = []
    for odd_row in range(2):
        for odd_time in range(2):
            for odd_col in range(2):
                taps = []
                for time_tap, source in (((0, 0), (2, 1)), ((1, 0),))[odd_time]:
                    for row_tap, row_step in SPACE_TAPS[odd_row]:
                        for col_tap, col_step in SPACE_TAPS[odd_col]:
                            index = (time_tap * 3 + row_tap) * 3 + col_tap
                            taps.append((index, source * 2 + col_step, row_step))
                order.append((odd_time, odd_row, odd_col, taps))
    weight_copies = {}
    for *_, taps in order:
        for index, *_ in taps:
            weight_copies[index] = pltpu.make_async_copy(
                weight_hbm.at[index], weight.at[index], weight_sems.at[index]
            )
            weight_copies[index].start()
    mean = stats_ref[0:1, :]
    factor = gain_ref[...] * lax.rsqrt(stats_ref[1:2, :] * (1.0 / count) + EPS)
    col = lax.broadcasted_iota(jnp.int32, (cols, width), 0)
    for source, ref in enumerate((current_ref, earlier_ref)):
        for row in range(3):
            value = (ref[row * cols : (row + 1) * cols, :].astype(F32) - mean) * factor + shift_ref[...]
            value = value / (1.0 + jnp.exp(-value))
            kept = (valid_ref[0] if row == 2 else 1) * (valid_ref[1] if source else 1)
            value = jnp.where(kept > 0, value, 0.0)
            place = slice(row * cols, (row + 1) * cols)
            active[2 * source, place, :] = value.astype(BF16)
            moved = jnp.where(col == cols - 1, 0.0, pltpu.roll(value, cols - 1, 0))
            active[2 * source + 1, place, :] = moved.astype(BF16)
    out_copies = []
    for odd_time, odd_row, odd_col, taps in order:
        for index, *_ in taps:
            weight_copies[index].wait()
        windows = [
            active[which, row_step * cols : (row_step + 2) * cols, :] for _, which, row_step in taps
        ]
        stacked = [weight[index] for index, *_ in taps]
        summed = jnp.dot(
            jnp.concatenate(windows, axis=1),
            jnp.concatenate(stacked, axis=0),
            preferred_element_type=F32,
        )
        summed = summed + bias_ref[...]
        for row in range(2):
            for lane in range(width // 128):
                wide[row, lane, pl.ds(odd_col, cols, stride=2), :] = summed[
                    row * cols : (row + 1) * cols, lane * 128 : (lane + 1) * 128
                ]
        if odd_col == 1:
            for row in range(2):
                for lane in range(width // 128):
                    out[odd_time, 2 * row + odd_row, :, lane * 128 : (lane + 1) * 128] = wide[
                        row, lane
                    ].astype(BF16)
                copy = pltpu.make_async_copy(
                    out.at[odd_time, 2 * row + odd_row],
                    out_hbm.at[odd_time, 2 * row + odd_row],
                    out_sems.at[odd_time, 2 * row + odd_row],
                )
                copy.start()
                out_copies.append(copy)
    for copy in out_copies:
        copy.wait()


def upsample(valid, current, earlier, stats, count, gain, shift, bias, weight):
    positions, width = current.shape
    cols = positions // 3
    vmem = pl.BlockSpec(memory_space=pltpu.VMEM)
    taps = weight.shape[0]
    return pl.pallas_call(
        functools.partial(upsample_kernel, count),
        out_shape=jax.ShapeDtypeStruct((2, 4, 2 * cols, width), BF16),
        in_specs=[pl.BlockSpec(memory_space=pltpu.SMEM)]
        + [vmem] * 6
        + [pl.BlockSpec(memory_space=pl.ANY)],
        out_specs=pl.BlockSpec(memory_space=pl.ANY),
        scratch_shapes=[
            pltpu.VMEM((4, positions, width), BF16),
            pltpu.VMEM((taps, width, width), BF16),
            pltpu.VMEM((2, width // 128, 2 * cols, 128), F32),
            pltpu.VMEM((2, 4, 2 * cols, width), BF16),
            pltpu.SemaphoreType.DMA((taps,)),
            pltpu.SemaphoreType.DMA((2, 4)),
        ],
        compiler_params=pltpu.CompilerParams(vmem_limit_bytes=VMEM_LIMIT),
        name="upsample",
    )(valid, current, earlier, stats, gain, shift, bias, weight)


def local(
    latent,
    first_gain,
    first_shift,
    query_weight,
    key_weight,
    value_weight,
    out_weight,
    out_bias,
    second_gain,
    second_shift,
    up_weight,
    up_bias,
):
    frames, rows, cols, width = latent.shape
    positions = rows * cols
    height, groups = lax.axis_size("height"), lax.axis_size("frames")
    slab, group = lax.axis_index("height"), lax.axis_index("frames")
    entries = positions * (width // GROUPS)
    count = entries * height * groups
    same_group = group_matrix(width)
    block = latent.reshape(positions, width)

    def summed_over_mesh(stats):
        held = entries
        for axis, size in (("height", height), ("frames", groups)):
            mask = 1
            while mask < size:
                stats = merged(stats, swapped(stats, axis, mask), held)
                held, mask = 2 * held, 2 * mask
        return stats

    slots = {0: block}
    masks = sorted(range(2, height, 2), key=lambda m: (bin(m).count("1"), -m))
    for mask in masks:
        lowest = mask & -mask
        slots[mask] = swapped(slots[mask ^ lowest], "height", lowest)
    for mask in [0] + masks:
        slots[mask | 1] = swapped(slots[mask], "height", 1)
    below = jnp.where(slab + 1 < height, slab ^ (slab + 1), 0).astype(jnp.int32).reshape(1)

    first = summed_over_mesh(local_stats(block, same_group))
    qk = lax.dot_general(
        query_weight, key_weight, (((1,), (1,)), ((), ())), preferred_element_type=F32
    ).astype(BF16)
    vo = jnp.dot(value_weight, out_weight, preferred_element_type=F32).astype(BF16)
    row = lambda vector: vector.reshape(1, width)
    mixed, second = attention(
        [slots[m] for m in range(height)],
        below,
        first,
        count,
        row(first_gain),
        row(first_shift),
        qk,
        vo,
        row(out_bias),
        same_group,
    )
    earlier = lax.ppermute(mixed, "frames", [(i, i + 1) for i in range(groups - 1)])
    second = summed_over_mesh(second)
    valid = jnp.stack([slab + 1 < height, group > 0]).astype(jnp.int32)
    result = upsample(
        valid,
        mixed,
        earlier,
        second,
        count,
        row(second_gain),
        row(second_shift),
        row(up_bias),
        up_weight.reshape(27, width, width),
    )
    return result


def solution(mesh):
    placed = P("frames", "height", None, None)
    return jax.shard_map(
        local,
        mesh=mesh,
        in_specs=(placed,) + (P(),) * 11,
        out_specs=placed,
        check_vma=False,
    )
```

```python
import functools
import math

import jax
import jax.numpy as jnp
import numpy as np
from jax import lax
from jax.experimental import pallas as pl
from jax.experimental.pallas import tpu as pltpu
from jax.sharding import PartitionSpec as P

GROUPS = 32
EPS = 1e-05
F32 = jnp.float32
BF16 = jnp.bfloat16
VMEM_LIMIT = 48 * 1024 * 1024


def swapped(value, axis, mask):
    count = lax.axis_size(axis)
    return lax.ppermute(value, axis, [(i, i ^ mask) for i in range(count)])


def group_sums(rows):
    width = rows[0].shape[1]
    row = lax.broadcasted_iota(jnp.int32, (8 * len(rows), width), 0)
    parts = jnp.zeros((8 * len(rows), width), F32)
    for i, rest in enumerate(rows):
        for j in range(3):
            part = rest.astype(BF16).astype(F32)
            rest = rest - part
            parts = jnp.where(row == 8 * i + j, part, parts)
    per_group = width // GROUPS
    groups = [
        jnp.floor((lax.broadcasted_iota(jnp.int32, (width, width), d).astype(F32) + 0.5) * (1.0 / per_group))
        for d in range(2)
    ]
    same_group = jnp.where(groups[0] == groups[1], 1.0, 0.0).astype(BF16)
    summed = jnp.dot(parts.astype(BF16), same_group, preferred_element_type=F32)
    return [jnp.sum(summed[8 * i : 8 * i + 8], axis=0, keepdims=True) for i in range(len(rows))]


def mean_and_spread(blocks):
    count = len(blocks) * blocks[0].shape[0]
    mean = sum(jnp.sum(b, axis=0, keepdims=True) for b in blocks) * (1.0 / count)
    return mean, sum(jnp.sum(jnp.square(b - mean), axis=0, keepdims=True) for b in blocks)


def group_mean_and_variance(means, spread, count):
    per_group = means.shape[1] // GROUPS
    mean = group_sums([means])[0] * (1.0 / per_group)
    gap = means - mean
    total = group_sums([spread + gap * gap * count])[0]
    return mean, total * (1.0 / (per_group * count))


def stats_kernel(own_hbm, other_ref, out_ref, own, sem):
    copy = pltpu.make_async_copy(own_hbm, own, sem)
    copy.start()
    copy.wait()
    mean, spread = mean_and_spread([own[...].astype(F32), other_ref[...].astype(F32)])
    for i in range(out_ref.shape[0]):
        out_ref[i, 0:1, :] = mean
        out_ref[i, 1:2, :] = spread


def local_stats(own, other, copies):
    vmem = pl.BlockSpec(memory_space=pltpu.VMEM)
    return pl.pallas_call(
        stats_kernel,
        out_shape=jax.ShapeDtypeStruct((copies, 2, own.shape[1]), F32),
        in_specs=[pl.BlockSpec(memory_space=pltpu.HBM), vmem],
        out_specs=vmem,
        scratch_shapes=[pltpu.VMEM(own.shape, own.dtype), pltpu.SemaphoreType.DMA],
        cost_estimate=pl.CostEstimate(flops=1 << 20, bytes_accessed=0, transcendentals=0),
        name="local_stats",
    )(own, other)


def prepare_kernel(query_ref, key_ref, value_ref, mix_ref, *refs):
    *vector_refs, qk_ref, vo_ref, vectors_ref = refs
    width = query_ref.shape[0]
    qk_ref[...] = lax.dot_general(
        query_ref[...], key_ref[...], (((1,), (1,)), ((), ())), preferred_element_type=F32
    ).astype(BF16)
    vo_ref[...] = jnp.dot(value_ref[...], mix_ref[...], preferred_element_type=F32).astype(BF16)
    for i, ref in enumerate(vector_refs):
        vectors_ref[i : i + 1, :] = ref[...].reshape(1, width)


def prepare(query, key, value, mix, *vectors):
    square = jax.ShapeDtypeStruct(query.shape, BF16)
    return pl.pallas_call(
        prepare_kernel,
        out_shape=(square, square, jax.ShapeDtypeStruct((len(vectors), query.shape[0]), F32)),
        cost_estimate=pl.CostEstimate(flops=4 * query.shape[0] ** 3, bytes_accessed=0, transcendentals=0),
        name="prepare",
    )(query, key, value, mix, *vectors)


def merged(stats, count):
    mean = jnp.mean(stats[:, 0], axis=0, keepdims=True)
    gap = stats[:, 0] - mean
    return mean, jnp.sum(stats[:, 1] + gap * gap * count, axis=0, keepdims=True)


def attention_kernel(starts, count, below_ref, stats_ref, qk_ref, vo_ref, vectors_ref, *refs):
    blocks = refs[: len(starts)]
    mixed_ref, out_stats_ref, keys, sems = refs[len(starts) :]
    positions, width = blocks[0].shape
    cols = positions // 2
    copies = [
        pltpu.make_async_copy(
            block, keys.at[pl.ds(start, block.shape[0]), :], sems.at[i]
        )
        for i, (start, block) in enumerate(zip(starts, blocks))
    ]
    for copy in copies:
        copy.start()
    mean, variance = group_mean_and_variance(stats_ref[0:1, :], stats_ref[1:2, :], count)
    gain, shift, bias = (vectors_ref[i : i + 1, :] for i in range(3))
    factor = gain * lax.rsqrt(variance + EPS)
    offset = shift - mean * factor
    scale = width ** (-0.5) * math.log2(math.e)
    for copy in copies:
        copy.wait()
    below = pl.multiple_of(below_ref[0] * positions, positions)
    for row in range(3):
        if row < 2:
            own = keys[row * cols : (row + 1) * cols, :].astype(F32)
        else:
            own = keys[pl.ds(below, cols), :].astype(F32)
        normed = ((own - mean) * factor + shift).astype(BF16)
        turned = jnp.dot(normed, qk_ref[...], preferred_element_type=F32) * scale
        constant = jnp.sum(turned * offset, axis=1, keepdims=True)
        queries = (turned * factor).astype(BF16)
        scores = lax.dot_general(
            queries, keys[...], (((1,), (1,)), ((), ())), preferred_element_type=F32
        )
        highest = jnp.max(scores, axis=1, keepdims=True) + constant
        probs = jnp.exp2(scores + (constant - highest)).astype(BF16)
        total = jnp.sum(probs.astype(F32), axis=1, keepdims=True)
        summed = jnp.dot(probs, keys[...], preferred_element_type=F32)
        attended = ((summed / total - mean) * factor + shift).astype(BF16)
        branch = jnp.dot(attended, vo_ref[...], preferred_element_type=F32) + bias
        mixed_ref[row * cols : (row + 1) * cols, :] = (own + branch).astype(BF16)
    mean, spread = mean_and_spread([mixed_ref[0:positions, :].astype(F32)])
    for i in range(out_stats_ref.shape[0]):
        out_stats_ref[i, 0:1, :] = mean
        out_stats_ref[i, 1:2, :] = spread


def attention(blocks, below, stats, count, qk, vo, vectors, stat_copies):
    starts, blocks = zip(*blocks)
    positions, width = blocks[0].shape
    vmem = pl.BlockSpec(memory_space=pltpu.VMEM)
    return pl.pallas_call(
        functools.partial(attention_kernel, starts, count),
        out_shape=(
            jax.ShapeDtypeStruct((positions // 2 * 3, width), BF16),
            jax.ShapeDtypeStruct((stat_copies, 2, width), F32),
        ),
        in_specs=[pl.BlockSpec(memory_space=pltpu.SMEM)]
        + [vmem] * 4
        + [pl.BlockSpec(memory_space=pltpu.HBM)]
        + [pl.BlockSpec(memory_space=pl.ANY)] * (len(blocks) - 1),
        out_specs=(vmem, vmem),
        scratch_shapes=[
            pltpu.VMEM((sum(b.shape[0] for b in blocks), width), BF16),
            pltpu.SemaphoreType.DMA((len(blocks),)),
        ],
        compiler_params=pltpu.CompilerParams(vmem_limit_bytes=VMEM_LIMIT),
        name="attention",
    )(below, stats, qk, vo, vectors, *blocks)


SPACE_TAPS = (((1, 0),), ((2, 0), (0, 1)))


def upsample_kernel(count, valid_ref, current_ref, earlier_ref, stats_ref, vectors_ref, weight_hbm, out_hbm, active, weight, wide, out, weight_sems, out_sems):
    positions, width = current_ref.shape
    cols = positions // 3
    order = []
    for odd_row in range(2):
        for odd_time in range(2):
            for odd_col in range(2):
                taps = []
                for time_tap, source in (((0, 0), (2, 1)), ((1, 0),))[odd_time]:
                    for row_tap, row_step in SPACE_TAPS[odd_row]:
                        for col_tap, col_step in SPACE_TAPS[odd_col]:
                            index = (time_tap * 3 + row_tap) * 3 + col_tap
                            taps.append((index, source * 2 + col_step, row_step))
                order.append((odd_time, odd_row, odd_col, taps))
    weight_copies = {}
    for *_, taps in order:
        for index, *_ in taps:
            weight_copies[index] = pltpu.make_async_copy(
                weight_hbm.at[index], weight.at[index], weight_sems.at[index]
            )
            weight_copies[index].start()
    mean, variance = group_mean_and_variance(*merged(stats_ref[...], count // stats_ref.shape[0]), count)
    gain, shift, bias = (vectors_ref[i : i + 1, :] for i in range(3, 6))
    factor = gain * lax.rsqrt(variance + EPS)
    col = lax.broadcasted_iota(jnp.int32, (cols, width), 0)
    for source, ref in enumerate((current_ref, earlier_ref)):
        for row in range(3):
            value = (ref[row * cols : (row + 1) * cols, :].astype(F32) - mean) * factor + shift
            value = value / (1.0 + jnp.exp(-value))
            kept = (valid_ref[0] if row == 2 else 1) * (valid_ref[1] if source else 1)
            value = jnp.where(kept > 0, value, 0.0)
            place = slice(row * cols, (row + 1) * cols)
            active[2 * source, place, :] = value.astype(BF16)
            moved = jnp.where(col == cols - 1, 0.0, pltpu.roll(value, cols - 1, 0))
            active[2 * source + 1, place, :] = moved.astype(BF16)
    out_copies = []
    for odd_time, odd_row, odd_col, taps in order:
        for index, *_ in taps:
            weight_copies[index].wait()
        windows = [
            active[which, row_step * cols : (row_step + 2) * cols, :] for _, which, row_step in taps
        ]
        stacked = [weight[index] for index, *_ in taps]
        summed = jnp.dot(
            jnp.concatenate(windows, axis=1),
            jnp.concatenate(stacked, axis=0),
            preferred_element_type=F32,
        )
        summed = summed + bias
        for row in range(2):
            for lane in range(width // 128):
                wide[row, lane, pl.ds(odd_col, cols, stride=2), :] = summed[
                    row * cols : (row + 1) * cols, lane * 128 : (lane + 1) * 128
                ]
        if odd_col == 1:
            for row in range(2):
                for lane in range(width // 128):
                    out[odd_time, 2 * row + odd_row, :, lane * 128 : (lane + 1) * 128] = wide[
                        row, lane
                    ].astype(BF16)
                copy = pltpu.make_async_copy(
                    out.at[odd_time, 2 * row + odd_row],
                    out_hbm.at[odd_time, 2 * row + odd_row],
                    out_sems.at[odd_time, 2 * row + odd_row],
                )
                copy.start()
                out_copies.append(copy)
    for copy in out_copies:
        copy.wait()


def upsample(valid, current, earlier, stats, count, vectors, weight):
    positions, width = current.shape
    cols = positions // 3
    vmem = pl.BlockSpec(memory_space=pltpu.VMEM)
    taps = weight.shape[0]
    return pl.pallas_call(
        functools.partial(upsample_kernel, count),
        out_shape=jax.ShapeDtypeStruct((2, 4, 2 * cols, width), BF16),
        in_specs=[pl.BlockSpec(memory_space=pltpu.SMEM)]
        + [vmem] * 4
        + [pl.BlockSpec(memory_space=pltpu.HBM)],
        out_specs=pl.BlockSpec(memory_space=pl.ANY),
        scratch_shapes=[
            pltpu.VMEM((4, positions, width), BF16),
            pltpu.VMEM((taps, width, width), BF16),
            pltpu.VMEM((2, width // 128, 2 * cols, 128), F32),
            pltpu.VMEM((2, 4, 2 * cols, width), BF16),
            pltpu.SemaphoreType.DMA((taps,)),
            pltpu.SemaphoreType.DMA((2, 4)),
        ],
        compiler_params=pltpu.CompilerParams(vmem_limit_bytes=VMEM_LIMIT),
        name="upsample",
    )(valid, current, earlier, stats, vectors, weight)


def local(
    latent,
    first_gain,
    first_shift,
    query_weight,
    key_weight,
    value_weight,
    out_weight,
    out_bias,
    second_gain,
    second_shift,
    up_weight,
    up_bias,
):
    frames, rows, cols, width = latent.shape
    positions = rows * cols
    height, groups = lax.axis_size("height"), lax.axis_size("frames")
    slab, group = lax.axis_index("height"), lax.axis_index("frames")
    count = positions * height * groups
    block = latent.reshape(positions, width)

    slots = {0: block, 1: swapped(block, "height", 1)}
    direct = [1 << i for i in range(1, (height - 1).bit_length())][::-1]
    forwarded = sorted((m for m in range(2, height, 2) if m not in direct), key=lambda m: (bin(m).count("1"), -m))
    for mask in direct:
        slots[mask] = swapped(block, "height", mask)
    held = 2 * positions

    def early_work(own, other, *parameters):
        stats = local_stats(own, other, groups)
        stats = lax.all_to_all(stats, "frames", split_axis=0, concat_axis=0, tiled=True)
        return jnp.concatenate(merged(stats, held), axis=0), *prepare(*parameters)

    parameters = (query_weight, key_weight, value_weight, out_weight)
    parameters += (first_gain, first_shift, out_bias, second_gain, second_shift, up_bias)
    first, qk, vo, vectors = lax.cond(
        group < groups,
        early_work,
        lambda *arguments: jax.tree.map(
            lambda kind: jnp.zeros(kind.shape, kind.dtype), jax.eval_shape(early_work, *arguments)
        ),
        block,
        slots[1],
        *parameters,
    )
    held = held * groups
    ready = lax.optimization_barrier([slots[m] for m in direct])
    slots.update(zip(direct, ready))
    for mask in forwarded:
        lowest = mask & -mask
        slots[mask] = swapped(slots[mask ^ lowest], "height", lowest)
    for mask in direct:
        pair = jnp.stack([first, swapped(first, "height", mask)])
        first, held = jnp.concatenate(merged(pair, held), axis=0), held * 2
    for mask in direct + forwarded:
        slots[mask | 1] = swapped(slots[mask], "height", 1)
    below = jnp.where(slab + 1 < height, slab ^ (slab + 1), 0).astype(jnp.int32).reshape(1)

    mixed, second = attention(
        [(m * positions, slots[m]) for m in range(height)],
        below,
        first,
        count,
        qk,
        vo,
        vectors,
        groups * height,
    )
    earlier = lax.ppermute(mixed, "frames", [(i, i + 1) for i in range(groups - 1)])
    second = lax.all_to_all(second, ("frames", "height"), split_axis=0, concat_axis=0, tiled=True)
    valid = jnp.stack([slab + 1 < height, group > 0]).astype(jnp.int32)
    result = upsample(
        valid,
        mixed,
        earlier,
        second,
        count,
        vectors,
        up_weight.reshape(27, width, width),
    )
    return result


def solution(mesh):
    placed = P("frames", "height", None, None)
    return jax.shard_map(
        local,
        mesh=mesh,
        in_specs=(placed,) + (P(),) * 11,
        out_specs=placed,
        check_vma=False,
    )
```

```python
import functools
import math

import jax
import jax.numpy as jnp
import numpy as np
from jax import lax
from jax.experimental import pallas as pl
from jax.experimental.pallas import tpu as pltpu
from jax.sharding import PartitionSpec as P

GROUPS = 32
EPS = 1e-05
F32 = jnp.float32
BF16 = jnp.bfloat16
VMEM_LIMIT = 26 * 1024 * 1024
AT_ONCE = 8


def swapped(value, axis, mask):
    count = lax.axis_size(axis)
    return lax.ppermute(value, axis, [(i, i ^ mask) for i in range(count)])


def group_sum(vector, same_group):
    row = lax.broadcasted_iota(jnp.int32, (8, vector.shape[1]), 0)
    parts = jnp.zeros((8, vector.shape[1]), F32)
    for i in range(3):
        part = vector.astype(BF16).astype(F32)
        vector = vector - part
        parts = jnp.where(row == i, part, parts)
    summed = jnp.dot(parts.astype(BF16), same_group, preferred_element_type=F32)
    return jnp.sum(summed, axis=0, keepdims=True)


def mean_and_spread(blocks):
    count = len(blocks) * blocks[0].shape[0]
    mean = sum(jnp.sum(b, axis=0, keepdims=True) for b in blocks) * (1.0 / count)
    return mean, sum(jnp.sum(jnp.square(b - mean), axis=0, keepdims=True) for b in blocks)


def group_mean_and_variance(means, spread, count, same_group):
    per_group = means.shape[1] // GROUPS
    mean = group_sum(means, same_group) * (1.0 / per_group)
    gap = means - mean
    total = group_sum(spread + gap * gap * count, same_group)
    return mean, total * (1.0 / (per_group * count))


def stats_kernel(own_hbm, other_ref, out_ref, own_ref, sem):
    copy = pltpu.make_async_copy(own_hbm, own_ref, sem)
    copy.start()
    copy.wait()
    mean, spread = mean_and_spread([own_ref[...].astype(F32), other_ref[...].astype(F32)])
    for i in range(out_ref.shape[0]):
        out_ref[i, 0:1, :] = mean
        out_ref[i, 1:2, :] = spread


def local_stats(own, other, copies):
    vmem = pl.BlockSpec(memory_space=pltpu.VMEM)
    return pl.pallas_call(
        stats_kernel,
        out_shape=(
            jax.ShapeDtypeStruct((copies, 2, own.shape[1]), F32),
            jax.ShapeDtypeStruct(own.shape, own.dtype),
        ),
        in_specs=[pl.BlockSpec(memory_space=pl.ANY), vmem],
        out_specs=(vmem, vmem),
        scratch_shapes=[pltpu.SemaphoreType.DMA],
        cost_estimate=pl.CostEstimate(flops=1 << 20, bytes_accessed=0, transcendentals=0),
        name="local_stats",
    )(own, other)


SPACE_TAPS = (((1, 0),), ((2, 0), (0, 1)))


def prepare_kernel(query_ref, key_ref, value_ref, mix_ref, *refs):
    *vector_refs, qk_ref, vo_ref, vectors_ref, same_ref = refs
    width = query_ref.shape[0]
    qk_ref[...] = lax.dot_general(
        query_ref[...], key_ref[...], (((1,), (1,)), ((), ())), preferred_element_type=F32
    ).astype(BF16)
    vo_ref[...] = jnp.dot(value_ref[...], mix_ref[...], preferred_element_type=F32).astype(BF16)
    for i, ref in enumerate(vector_refs):
        vectors_ref[i : i + 1, :] = ref[...].reshape(1, width)
    groups = [
        jnp.floor((lax.broadcasted_iota(jnp.int32, (width, width), d).astype(F32) + 0.5) * (GROUPS / width))
        for d in range(2)
    ]
    same_ref[...] = jnp.where(groups[0] == groups[1], 1.0, 0.0).astype(BF16)


def prepare(query, key, value, mix, *vectors):
    square = jax.ShapeDtypeStruct(query.shape, BF16)
    return pl.pallas_call(
        prepare_kernel,
        out_shape=(square, square, jax.ShapeDtypeStruct((len(vectors), query.shape[0]), F32), square),
        cost_estimate=pl.CostEstimate(flops=4 * query.shape[0] ** 3, bytes_accessed=0, transcendentals=0),
        name="prepare",
    )(query, key, value, mix, *vectors)


def merged(stats, count):
    mean = jnp.mean(stats[:, 0], axis=0, keepdims=True)
    gap = stats[:, 0] - mean
    return mean, jnp.sum(stats[:, 1] + gap * gap * count, axis=0, keepdims=True)


def attention_kernel(count, distance_ref, stats_ref, qk_ref, vo_ref, vectors_ref, same_ref, *refs):
    *blocks, mixed_ref, out_stats_ref = refs
    positions, width = blocks[0].shape
    cols = positions // 2
    mean, variance = group_mean_and_variance(
        stats_ref[0:1, :], stats_ref[1:2, :], count, same_ref[...]
    )
    gain, shift, bias = (vectors_ref[i : i + 1, :] for i in range(3))
    factor = gain * lax.rsqrt(variance + EPS)
    offset = shift - mean * factor
    scale = width ** (-0.5) * math.log2(math.e)
    below = blocks[1][0:cols, :]
    mask = 3
    while mask < len(blocks):
        below = jnp.where(distance_ref[0] == mask, blocks[mask][0:cols, :], below)
        mask = 2 * mask + 1
    own = jnp.concatenate([blocks[0][...], below], axis=0).astype(F32)
    normed = ((own - mean) * factor + shift).astype(BF16)
    turned = jnp.dot(normed, qk_ref[...], preferred_element_type=F32) * scale
    constant = jnp.sum(turned * offset, axis=1, keepdims=True)
    queries = (turned * factor).astype(BF16)
    highest = None
    for first in range(0, len(blocks), AT_ONCE):
        keys = jnp.concatenate([block[...] for block in blocks[first : first + AT_ONCE]], axis=0)
        scores = lax.dot_general(
            queries, keys, (((1,), (1,)), ((), ())), preferred_element_type=F32
        )
        newest = jnp.max(scores, axis=1, keepdims=True) + constant
        if highest is not None:
            newest = jnp.maximum(highest, newest)
        probs = jnp.exp2(scores + (constant - newest)).astype(BF16)
        part = jnp.sum(probs.astype(F32), axis=1, keepdims=True)
        product = jnp.dot(probs, keys, preferred_element_type=F32)
        if highest is None:
            total, summed = part, product
        else:
            fade = jnp.exp2(highest - newest)
            total, summed = total * fade + part, summed * fade + product
        highest = newest
    attended = ((summed / total - mean) * factor + shift).astype(BF16)
    branch = jnp.dot(attended, vo_ref[...], preferred_element_type=F32) + bias
    mixed = (own + branch).astype(BF16)
    mixed_ref[...] = mixed
    mean, spread = mean_and_spread([mixed[:positions].astype(F32)])
    for i in range(out_stats_ref.shape[0]):
        out_stats_ref[i, 0:1, :] = mean
        out_stats_ref[i, 1:2, :] = spread


def attention(blocks, distance, stats, count, qk, vo, vectors, same_group, stat_copies):
    positions, width = blocks[0].shape
    vmem = pl.BlockSpec(memory_space=pltpu.VMEM)
    return pl.pallas_call(
        functools.partial(attention_kernel, count),
        out_shape=(
            jax.ShapeDtypeStruct((positions // 2 * 3, width), BF16),
            jax.ShapeDtypeStruct((stat_copies, 2, width), F32),
        ),
        in_specs=[pl.BlockSpec(memory_space=pltpu.SMEM)] + [vmem] * (5 + len(blocks)),
        out_specs=(vmem, vmem),
        compiler_params=pltpu.CompilerParams(vmem_limit_bytes=VMEM_LIMIT * (2 if len(blocks) > AT_ONCE else 1)),
        name="attention",
    )(distance, stats, qk, vo, vectors, same_group, *blocks)


def fetch_kernel(after, weight_hbm, middle_ref, sem):
    copy = pltpu.make_async_copy(weight_hbm.at[:, 1], middle_ref, sem)
    copy.start()
    copy.wait()


def fetch(after, weight):
    width = weight.shape[-1]
    anywhere = pl.BlockSpec(memory_space=pl.ANY)
    return pl.pallas_call(
        fetch_kernel,
        out_shape=pltpu.VMEM((3, 3, width, width), BF16),
        in_specs=[anywhere, anywhere],
        out_specs=pl.BlockSpec(memory_space=pltpu.VMEM),
        scratch_shapes=[pltpu.SemaphoreType.DMA],
        cost_estimate=pl.CostEstimate(flops=0, bytes_accessed=36 * width**2, transcendentals=0),
        compiler_params=pltpu.CompilerParams(vmem_limit_bytes=VMEM_LIMIT),
        name="fetch",
    )(after, pltpu.with_memory_space_constraint(weight, pltpu.HBM))


def upsample_kernel(count, valid_ref, current_ref, earlier_ref, stats_ref, vectors_ref, same_ref, middle_ref, weight_hbm, out_hbm, now, before, wide, out, weight, weight_sems, out_sems):
    positions, width = current_ref.shape
    cols = positions // 3
    copies = {
        r: pltpu.make_async_copy(weight_hbm.at[:, r], weight.at[:, r // 2], weight_sems.at[r // 2]) for r in (2, 0)
    }
    for copy in copies.values():
        copy.start()
    mean, variance = group_mean_and_variance(
        *merged(stats_ref[...], count // stats_ref.shape[0]), count, same_ref[...]
    )
    gain, shift, bias = (vectors_ref[i : i + 1, :] for i in range(3, 6))
    factor = gain * lax.rsqrt(variance + EPS)
    col = lax.broadcasted_iota(jnp.int32, (cols, width), 0)
    for target, source_ref, known in ((now, current_ref, None), (before, earlier_ref, valid_ref[1])):
        for row in range(3):
            source = source_ref[row * cols : (row + 1) * cols, :]
            value = (source.astype(F32) - mean) * factor + shift
            value = value / (1.0 + jnp.exp(-value))
            kept = known
            if row == 2:
                kept = valid_ref[0] if known is None else valid_ref[0] * known
            if kept is not None:
                value = jnp.where(kept > 0, value, 0.0)
            here = slice(row * cols, (row + 1) * cols)
            target[here, 0:width] = value.astype(BF16)
            moved = jnp.where(col == cols - 1, 0.0, pltpu.roll(value, cols - 1, 0))
            target[here, width : 2 * width] = moved.astype(BF16)
    out_copies = []

    def multiplied(odd_row, odd_col):
        taps = [(r, c) for r, _ in SPACE_TAPS[odd_row] for c, _ in SPACE_TAPS[odd_col]]

        def product(active, *times):
            lanes = slice(0, 2 * width if odd_col else width)
            windows = [active[step * cols : (step + 2) * cols, lanes] for _, step in SPACE_TAPS[odd_row]]
            stacked = [jnp.concatenate([(middle_ref[t, c] if r == 1 else weight[t, r // 2, c]) for t in times], axis=1) for r, c in taps]
            return jnp.dot(
                jnp.concatenate(windows, axis=1),
                jnp.concatenate(stacked, axis=0),
                preferred_element_type=F32,
            )

        both = product(now, 0, 1)
        return both[:, :width] + product(before, 2) + bias, both[:, width:] + bias

    def stored(odd_row, odd_col, sums):
        for odd_time, summed in enumerate(sums):
            for row in range(2):
                for lane in range(width // 128):
                    wide[odd_time, row, lane, pl.ds(odd_col, cols, stride=2), :] = summed[
                        row * cols : (row + 1) * cols, lane * 128 : (lane + 1) * 128
                    ]
                if odd_col == 1:
                    for lane in range(width // 128):
                        out[odd_time, row, odd_row, :, lane * 128 : (lane + 1) * 128] = wide[
                            odd_time, row, lane
                        ].astype(BF16)
            if odd_col == 1:
                place = (odd_time, slice(None), odd_row)
                copy = pltpu.make_async_copy(
                    out.at[*place], out_hbm.at[*place], out_sems.at[odd_time, odd_row]
                )
                copy.start()
                out_copies.append(copy)

    first = [(phase, multiplied(*phase)) for phase in ((0, 0), (0, 1))]
    stored(*first[0][0], first[0][1])
    for copy in copies.values():
        copy.wait()
    stored(*first[1][0], first[1][1])
    for phase in ((1, 0), (1, 1)):
        stored(*phase, multiplied(*phase))
    for copy in out_copies:
        copy.wait()


def upsample(valid, current, earlier, stats, count, vectors, same_group, middle, weight):
    positions, width = current.shape
    cols = positions // 3
    vmem = pl.BlockSpec(memory_space=pltpu.VMEM)
    result = pl.pallas_call(
        functools.partial(upsample_kernel, count),
        out_shape=jax.ShapeDtypeStruct((2, 2, 2, 2 * cols, width), BF16),
        in_specs=[pl.BlockSpec(memory_space=pltpu.SMEM)]
        + [vmem] * 6
        + [pl.BlockSpec(memory_space=pl.ANY)],
        out_specs=pl.BlockSpec(memory_space=pl.ANY),
        scratch_shapes=[
            pltpu.VMEM((3 * cols, 2 * width), BF16),
            pltpu.VMEM((3 * cols, 2 * width), BF16),
            pltpu.VMEM((2, 2, width // 128, 2 * cols, 128), F32),
            pltpu.VMEM((2, 2, 2, 2 * cols, width), BF16),
            pltpu.VMEM((3, 2, 3, width, width), BF16),
            pltpu.SemaphoreType.DMA((2,)),
            pltpu.SemaphoreType.DMA((2, 2)),
        ],
        compiler_params=pltpu.CompilerParams(vmem_limit_bytes=VMEM_LIMIT),
        name="upsample",
    )(
        valid, current, earlier, stats, vectors, same_group, middle, pltpu.with_memory_space_constraint(weight, pltpu.HBM)
    )
    return result.reshape(2, 4, 2 * cols, width)


def local(
    latent,
    first_gain,
    first_shift,
    query_weight,
    key_weight,
    value_weight,
    out_weight,
    out_bias,
    second_gain,
    second_shift,
    up_weight,
    up_bias,
):
    frames, rows, cols, width = latent.shape
    positions = rows * cols
    height, groups = lax.axis_size("height"), lax.axis_size("frames")
    slab, group = lax.axis_index("height"), lax.axis_index("frames")
    count = positions * height * groups
    block = latent.reshape(positions, width)

    slots = {0: block, 1: swapped(block, "height", 1)}
    direct = [1 << i for i in range(1, (height - 1).bit_length())][::-1]
    forwarded = sorted((m for m in range(2, height, 2) if m not in direct), key=lambda m: (bin(m).count("1"), -m))
    for mask in direct:
        slots[mask] = swapped(block, "height", mask)
    held = 2 * positions

    def early_work(own, other, *parameters):
        stats, own = local_stats(own, other, groups)
        stats = lax.all_to_all(stats, "frames", split_axis=0, concat_axis=0, tiled=True)
        return jnp.concatenate(merged(stats, held), axis=0), own, *prepare(*parameters)

    parameters = (query_weight, key_weight, value_weight, out_weight)
    parameters += (first_gain, first_shift, out_bias, second_gain, second_shift, up_bias)
    first, slots[0], qk, vo, vectors, same_group = lax.cond(
        group < groups,
        early_work,
        lambda *arguments: jax.tree.map(
            lambda kind: jnp.zeros(kind.shape, kind.dtype), jax.eval_shape(early_work, *arguments)
        ),
        block,
        slots[1],
        *parameters,
    )
    held = held * groups
    ready = lax.optimization_barrier([slots[m] for m in direct])
    slots.update(zip(direct, ready))
    for mask in forwarded:
        lowest = mask & -mask
        slots[mask] = swapped(slots[mask ^ lowest], "height", lowest)
    for mask in direct:
        pair = jnp.stack([first, swapped(first, "height", mask)])
        first, held = jnp.concatenate(merged(pair, held), axis=0), held * 2
    for mask in direct + forwarded:
        slots[mask | 1] = swapped(slots[mask], "height", 1)
    distance = (slab ^ (slab + 1)).astype(jnp.int32).reshape(1)

    blocks = [slots[m] for m in range(height)]
    mixed, second = attention(
        blocks, distance, first, count, qk, vo, vectors, same_group, groups * height
    )
    middle = fetch(mixed, up_weight)
    earlier = lax.ppermute(mixed, "frames", [(i, i + 1) for i in range(groups - 1)])
    second = lax.all_to_all(second, ("frames", "height"), split_axis=0, concat_axis=0, tiled=True)
    valid = jnp.stack([slab + 1 < height, group > 0]).astype(jnp.int32)
    return upsample(
        valid, mixed, earlier, second, count, vectors, same_group, middle, up_weight
    )


def solution(mesh):
    placed = P("frames", "height", None, None)
    return jax.shard_map(
        local,
        mesh=mesh,
        in_specs=(placed,) + (P(),) * 11,
        out_specs=placed,
        check_vma=False,
    )
```

```python
import functools
import math

import jax
import jax.numpy as jnp
import numpy as np
from jax import lax
from jax.experimental import pallas as pl
from jax.experimental.pallas import tpu as pltpu
from jax.sharding import PartitionSpec as P

GROUPS = 32
EPS = 1e-05
F32 = jnp.float32
BF16 = jnp.bfloat16
VMEM_LIMIT = 26 * 1024 * 1024
AT_ONCE = 8
LANES = 128


def swapped(value, axis, mask):
    count = lax.axis_size(axis)
    return lax.ppermute(value, axis, [(i, i ^ mask) for i in range(count)])


def exact_product(rows, matrix, contracted=0):
    row = lax.broadcasted_iota(jnp.int32, (8 * len(rows), rows[0].shape[1]), 0)
    parts = jnp.zeros(row.shape, F32)
    for i, rest in enumerate(rows):
        for j in range(3):
            part = rest.astype(BF16).astype(F32)
            rest = rest - part
            parts = jnp.where(row == 8 * i + j, part, parts)
    summed = lax.dot_general(
        parts.astype(BF16), matrix, (((1,), (contracted,)), ((), ())), preferred_element_type=F32
    )
    return [jnp.sum(summed[8 * i : 8 * i + 8], axis=0, keepdims=True) for i in range(len(rows))]


def mean_and_spread(blocks):
    count = len(blocks) * blocks[0].shape[0]
    mean = sum(jnp.sum(b, axis=0, keepdims=True) for b in blocks) * (1.0 / count)
    return mean, sum(jnp.sum(jnp.square(b - mean), axis=0, keepdims=True) for b in blocks)


def group_mean_and_spread(means, spread, count, same_group):
    mean = exact_product([means], same_group)[0] * (GROUPS / means.shape[1])
    gap = means - mean
    return mean, spread + gap * gap * count


def stats_kernel(own_hbm, other_ref, out_ref, own_ref, sem):
    copy = pltpu.make_async_copy(own_hbm, own_ref, sem)
    copy.start()
    copy.wait()
    mean, spread = mean_and_spread([own_ref[...].astype(F32), other_ref[...].astype(F32)])
    for i in range(out_ref.shape[0]):
        out_ref[i, 0:1, :] = mean
        out_ref[i, 1:2, :] = spread


def local_stats(own, other, copies):
    vmem = pl.BlockSpec(memory_space=pltpu.VMEM)
    return pl.pallas_call(
        stats_kernel,
        out_shape=(
            jax.ShapeDtypeStruct((copies, 2, own.shape[1]), F32),
            jax.ShapeDtypeStruct(own.shape, own.dtype),
        ),
        in_specs=[pl.BlockSpec(memory_space=pl.ANY), vmem],
        out_specs=(vmem, vmem),
        scratch_shapes=[pltpu.SemaphoreType.DMA],
        cost_estimate=pl.CostEstimate(flops=1 << 20, bytes_accessed=0, transcendentals=0),
        name="local_stats",
    )(own, other)


SPACE_TAPS = (((1, 0),), ((2, 0), (0, 1)))


def prepare_kernel(query_ref, key_ref, value_ref, mix_ref, *refs):
    *vector_refs, qk_ref, vo_ref, vectors_ref, same_ref, member_ref = refs
    width = query_ref.shape[0]
    qk_ref[...] = lax.dot_general(
        query_ref[...], key_ref[...], (((1,), (1,)), ((), ())), preferred_element_type=F32
    ).astype(BF16)
    vo_ref[...] = jnp.dot(value_ref[...], mix_ref[...], preferred_element_type=F32).astype(BF16)
    for i, ref in enumerate(vector_refs):
        vectors_ref[i : i + 1, :] = ref[...].reshape(1, width)
    group = lambda dim: jnp.floor(
        (lax.broadcasted_iota(jnp.int32, (width, width), dim).astype(F32) + 0.5) * (GROUPS / width)
    )
    same_ref[...] = jnp.where(group(0) == group(1), 1.0, 0.0).astype(BF16)
    lane = lax.broadcasted_iota(jnp.int32, member_ref.shape, 1).astype(F32)
    member_ref[...] = jnp.where(group(0)[:, :LANES] == lane, 1.0, 0.0).astype(BF16)


def prepare(query, key, value, mix, *vectors):
    square = jax.ShapeDtypeStruct(query.shape, BF16)
    return pl.pallas_call(
        prepare_kernel,
        out_shape=(
            square,
            square,
            jax.ShapeDtypeStruct((len(vectors), query.shape[0]), F32),
            square,
            jax.ShapeDtypeStruct((query.shape[0], LANES), BF16),
        ),
        cost_estimate=pl.CostEstimate(flops=4 * query.shape[0] ** 3, bytes_accessed=0, transcendentals=0),
        name="prepare",
    )(query, key, value, mix, *vectors)


def merged(stats, count):
    mean = jnp.mean(stats[:, 0], axis=0, keepdims=True)
    gap = stats[:, 0] - mean
    return mean, jnp.sum(stats[:, 1] + gap * gap * count, axis=0, keepdims=True)


def attention_kernel(count, distance_ref, stats_ref, qk_ref, vo_ref, vectors_ref, same_ref, member_ref, *refs):
    *blocks, mixed_ref, out_stats_ref = refs
    positions, width = blocks[0].shape
    cols = positions // 2
    mean, spread = group_mean_and_spread(
        stats_ref[0:1, :], stats_ref[1:2, :], count, same_ref[...]
    )
    variance = exact_product([spread], same_ref[...])[0] * (GROUPS / (width * count))
    gain, shift, bias = (vectors_ref[i : i + 1, :] for i in range(3))
    factor = gain * lax.rsqrt(variance + EPS)
    offset = shift - mean * factor
    scale = width ** (-0.5) * math.log2(math.e)
    below = blocks[1][0:cols, :]
    mask = 3
    while mask < len(blocks):
        below = jnp.where(distance_ref[0] == mask, blocks[mask][0:cols, :], below)
        mask = 2 * mask + 1
    own = jnp.concatenate([blocks[0][...], below], axis=0).astype(F32)
    normed = ((own - mean) * factor + shift).astype(BF16)
    turned = jnp.dot(normed, qk_ref[...], preferred_element_type=F32) * scale
    constant = jnp.sum(turned * offset, axis=1, keepdims=True)
    queries = (turned * factor).astype(BF16)
    highest = None
    for first in range(0, len(blocks), AT_ONCE):
        keys = jnp.concatenate([block[...] for block in blocks[first : first + AT_ONCE]], axis=0)
        scores = lax.dot_general(
            queries, keys, (((1,), (1,)), ((), ())), preferred_element_type=F32
        )
        newest = jnp.max(scores, axis=1, keepdims=True) + constant
        if highest is not None:
            newest = jnp.maximum(highest, newest)
        probs = jnp.exp2(scores + (constant - newest)).astype(BF16)
        wide_keys = jnp.concatenate([keys, jnp.ones((keys.shape[0], 128), BF16)], axis=1)
        product = jnp.dot(probs, wide_keys, preferred_element_type=F32)
        product, part = product[:, :width], product[:, width : width + 1]
        if highest is None:
            total, summed = part, product
        else:
            fade = jnp.exp2(highest - newest)
            total, summed = total * fade + part, summed * fade + product
        highest = newest
    attended = ((summed / total - mean) * factor + shift).astype(BF16)
    branch = jnp.dot(attended, vo_ref[...], preferred_element_type=F32) + bias
    mixed = (own + branch).astype(BF16)
    mixed_ref[...] = mixed
    mean, spread = mean_and_spread([mixed[:positions].astype(F32)])
    _, group_spread = group_mean_and_spread(mean, spread, positions, same_ref[...])
    mean, spread = exact_product([mean * (GROUPS / width), group_spread], member_ref[...])
    for i in range(out_stats_ref.shape[0]):
        out_stats_ref[i, 0:1, :] = mean
        out_stats_ref[i, 1:2, :] = spread


def attention(blocks, distance, stats, count, qk, vo, vectors, same_group, member, stat_copies):
    positions, width = blocks[0].shape
    vmem = pl.BlockSpec(memory_space=pltpu.VMEM)
    return pl.pallas_call(
        functools.partial(attention_kernel, count),
        out_shape=(
            jax.ShapeDtypeStruct((positions // 2 * 3, width), BF16),
            jax.ShapeDtypeStruct((stat_copies, 2, LANES), F32),
        ),
        in_specs=[pl.BlockSpec(memory_space=pltpu.SMEM)] + [vmem] * (6 + len(blocks)),
        out_specs=(vmem, vmem),
        compiler_params=pltpu.CompilerParams(vmem_limit_bytes=VMEM_LIMIT * (2 if len(blocks) > AT_ONCE else 1)),
        name="attention",
    )(distance, stats, qk, vo, vectors, same_group, member, *blocks)


def fetch_kernel(after, weight_hbm, middle_ref, sem):
    copy = pltpu.make_async_copy(weight_hbm.at[:, 1], middle_ref, sem)
    copy.start()
    copy.wait()


def fetch(after, weight):
    width = weight.shape[-1]
    anywhere = pl.BlockSpec(memory_space=pl.ANY)
    return pl.pallas_call(
        fetch_kernel,
        out_shape=pltpu.VMEM((3, 3, width, width), BF16),
        in_specs=[anywhere, anywhere],
        out_specs=pl.BlockSpec(memory_space=pltpu.VMEM),
        scratch_shapes=[pltpu.SemaphoreType.DMA],
        cost_estimate=pl.CostEstimate(flops=0, bytes_accessed=36 * width**2, transcendentals=0),
        compiler_params=pltpu.CompilerParams(vmem_limit_bytes=VMEM_LIMIT),
        name="fetch",
    )(after, pltpu.with_memory_space_constraint(weight, pltpu.HBM))


def upsample_kernel(count, valid_ref, current_ref, earlier_ref, stats_ref, vectors_ref, member_ref, middle_ref, weight_hbm, out_hbm, now, before, wide, out, weight, weight_sems, out_sems):
    positions, width = current_ref.shape
    cols = positions // 3
    copies = {
        r: pltpu.make_async_copy(weight_hbm.at[:, r], weight.at[:, r // 2], weight_sems.at[r // 2]) for r in (2, 0)
    }
    for copy in copies.values():
        copy.start()
    entries = count * width // GROUPS
    mean, spread = merged(stats_ref[...], entries // stats_ref.shape[0])
    mean, variance = exact_product([mean, spread * (1.0 / entries)], member_ref[...], 1)
    gain, shift, bias = (vectors_ref[i : i + 1, :] for i in range(3, 6))
    factor = gain * lax.rsqrt(variance + EPS)
    col = lax.broadcasted_iota(jnp.int32, (cols, width), 0)
    for target, source_ref, known in ((now, current_ref, None), (before, earlier_ref, valid_ref[1])):
        for row in range(3):
            source = source_ref[row * cols : (row + 1) * cols, :]
            value = (source.astype(F32) - mean) * factor + shift
            value = value / (1.0 + jnp.exp(-value))
            kept = known
            if row == 2:
                kept = valid_ref[0] if known is None else valid_ref[0] * known
            if kept is not None:
                value = jnp.where(kept > 0, value, 0.0)
            here = slice(row * cols, (row + 1) * cols)
            target[here, 0:width] = value.astype(BF16)
            moved = jnp.where(col == cols - 1, 0.0, pltpu.roll(value, cols - 1, 0))
            target[here, width : 2 * width] = moved.astype(BF16)
    out_copies = []

    def multiplied(odd_row, odd_col):
        taps = [(r, c) for r, _ in SPACE_TAPS[odd_row] for c, _ in SPACE_TAPS[odd_col]]

        def product(active, *times):
            lanes = slice(0, 2 * width if odd_col else width)
            windows = [active[step * cols : (step + 2) * cols, lanes] for _, step in SPACE_TAPS[odd_row]]
            stacked = [jnp.concatenate([(middle_ref[t, c] if r == 1 else weight[t, r // 2, c]) for t in times], axis=1) for r, c in taps]
            return jnp.dot(
                jnp.concatenate(windows, axis=1),
                jnp.concatenate(stacked, axis=0),
                preferred_element_type=F32,
            )

        both = product(now, 0, 1)
        return both[:, :width] + product(before, 2) + bias, both[:, width:] + bias

    def stored(odd_row, odd_col, sums):
        for odd_time, summed in enumerate(sums):
            for row in range(2):
                for lane in range(width // 128):
                    wide[odd_time, row, lane, pl.ds(odd_col, cols, stride=2), :] = summed[
                        row * cols : (row + 1) * cols, lane * 128 : (lane + 1) * 128
                    ]
                if odd_col == 1:
                    for lane in range(width // 128):
                        out[odd_time, row, odd_row, :, lane * 128 : (lane + 1) * 128] = wide[
                            odd_time, row, lane
                        ].astype(BF16)
            if odd_col == 1:
                place = (odd_time, slice(None), odd_row)
                copy = pltpu.make_async_copy(
                    out.at[*place], out_hbm.at[*place], out_sems.at[odd_time, odd_row]
                )
                copy.start()
                out_copies.append(copy)

    first = [(phase, multiplied(*phase)) for phase in ((0, 0), (0, 1))]
    stored(*first[0][0], first[0][1])
    stored(*first[1][0], first[1][1])
    for copy in copies.values():
        copy.wait()
    for phase in ((1, 0), (1, 1)):
        stored(*phase, multiplied(*phase))
    for copy in out_copies:
        copy.wait()


def upsample(valid, current, earlier, stats, count, vectors, member, middle, weight):
    positions, width = current.shape
    cols = positions // 3
    vmem = pl.BlockSpec(memory_space=pltpu.VMEM)
    result = pl.pallas_call(
        functools.partial(upsample_kernel, count),
        out_shape=jax.ShapeDtypeStruct((2, 2, 2, 2 * cols, width), BF16),
        in_specs=[pl.BlockSpec(memory_space=pltpu.SMEM)]
        + [vmem] * 6
        + [pl.BlockSpec(memory_space=pl.ANY)],
        out_specs=pl.BlockSpec(memory_space=pl.ANY),
        scratch_shapes=[
            pltpu.VMEM((3 * cols, 2 * width), BF16),
            pltpu.VMEM((3 * cols, 2 * width), BF16),
            pltpu.VMEM((2, 2, width // 128, 2 * cols, 128), F32),
            pltpu.VMEM((2, 2, 2, 2 * cols, width), BF16),
            pltpu.VMEM((3, 2, 3, width, width), BF16),
            pltpu.SemaphoreType.DMA((2,)),
            pltpu.SemaphoreType.DMA((2, 2)),
        ],
        compiler_params=pltpu.CompilerParams(vmem_limit_bytes=VMEM_LIMIT),
        name="upsample",
    )(
        valid, current, earlier, stats, vectors, member, middle, pltpu.with_memory_space_constraint(weight, pltpu.HBM)
    )
    return result.reshape(2, 4, 2 * cols, width)


def local(
    latent,
    first_gain,
    first_shift,
    query_weight,
    key_weight,
    value_weight,
    out_weight,
    out_bias,
    second_gain,
    second_shift,
    up_weight,
    up_bias,
):
    frames, rows, cols, width = latent.shape
    positions = rows * cols
    height, groups = lax.axis_size("height"), lax.axis_size("frames")
    slab, group = lax.axis_index("height"), lax.axis_index("frames")
    count = positions * height * groups
    block = latent.reshape(positions, width)

    slots = {0: block, 1: swapped(block, "height", 1)}
    direct = [1 << i for i in range(1, (height - 1).bit_length())]
    forwarded = sorted((m for m in range(2, height, 2) if m not in direct), key=lambda m: (bin(m).count("1"), -m))
    for mask in direct:
        slots[mask] = swapped(block, "height", mask)
    held = 2 * positions

    def early_work(own, other, *parameters):
        stats, own = local_stats(own, other, groups)
        stats = lax.all_to_all(stats, "frames", split_axis=0, concat_axis=0, tiled=True)
        return jnp.concatenate(merged(stats, held), axis=0), own, *prepare(*parameters)

    parameters = (query_weight, key_weight, value_weight, out_weight)
    parameters += (first_gain, first_shift, out_bias, second_gain, second_shift, up_bias)
    first, slots[0], qk, vo, vectors, same_group, member = lax.cond(
        group < groups,
        early_work,
        lambda *arguments: jax.tree.map(
            lambda kind: jnp.zeros(kind.shape, kind.dtype), jax.eval_shape(early_work, *arguments)
        ),
        block,
        slots[1],
        *parameters,
    )
    held = held * groups
    _, *ready = lax.optimization_barrier([first] + [slots[m] for m in direct])
    slots.update(zip(direct, ready))
    for mask in forwarded:
        lowest = mask & -mask
        slots[mask] = swapped(slots[mask ^ lowest], "height", lowest)
    for mask in direct:
        pair = jnp.stack([first, swapped(first, "height", mask)])
        first, held = jnp.concatenate(merged(pair, held), axis=0), held * 2
    for mask in direct + forwarded:
        slots[mask | 1] = swapped(slots[mask], "height", 1)
    distance = (slab ^ (slab + 1)).astype(jnp.int32).reshape(1)

    blocks = [slots[m] for m in range(height)]
    mixed, second = attention(
        blocks, distance, first, count, qk, vo, vectors, same_group, member, groups * height
    )
    middle = fetch(mixed, up_weight)
    earlier = lax.ppermute(mixed, "frames", [(i, i + 1) for i in range(groups - 1)])
    second = lax.all_to_all(second, ("frames", "height"), split_axis=0, concat_axis=0, tiled=True)
    valid = jnp.stack([slab + 1 < height, group > 0]).astype(jnp.int32)
    return upsample(
        valid, mixed, earlier, second, count, vectors, member, middle, up_weight
    )


def solution(mesh):
    placed = P("frames", "height", None, None)
    return jax.shard_map(
        local,
        mesh=mesh,
        in_specs=(placed,) + (P(),) * 11,
        out_specs=placed,
        check_vma=False,
    )
```

```python
import functools
import math

import jax
import jax.numpy as jnp
import numpy as np
from jax import lax
from jax.experimental import pallas as pl
from jax.experimental.pallas import tpu as pltpu
from jax.sharding import PartitionSpec as P

GROUPS = 32
EPS = 1e-05
F32 = jnp.float32
BF16 = jnp.bfloat16
VMEM_LIMIT = 26 * 1024 * 1024
AT_ONCE = 8
LANES = 128


def swapped(value, axis, mask):
    count = lax.axis_size(axis)
    return lax.ppermute(value, axis, [(i, i ^ mask) for i in range(count)])


def exact_product(rows, matrix, contracted=0):
    row = lax.broadcasted_iota(jnp.int32, (8 * len(rows), rows[0].shape[1]), 0)
    parts = jnp.zeros(row.shape, F32)
    for i, rest in enumerate(rows):
        for j in range(3):
            part = rest.astype(BF16).astype(F32)
            rest = rest - part
            parts = jnp.where(row == 8 * i + j, part, parts)
    summed = lax.dot_general(
        parts.astype(BF16), matrix, (((1,), (contracted,)), ((), ())), preferred_element_type=F32
    )
    return [jnp.sum(summed[8 * i : 8 * i + 8], axis=0, keepdims=True) for i in range(len(rows))]


def mean_and_spread(blocks):
    count = len(blocks) * blocks[0].shape[0]
    mean = sum(jnp.sum(b, axis=0, keepdims=True) for b in blocks) * (1.0 / count)
    return mean, sum(jnp.sum(jnp.square(b - mean), axis=0, keepdims=True) for b in blocks)


def group_mean_and_spread(means, spread, count, same_group):
    mean = exact_product([means], same_group)[0] * (GROUPS / means.shape[1])
    gap = means - mean
    return mean, spread + gap * gap * count


def stats_kernel(own_hbm, other_ref, out_ref, own_ref, sem):
    copy = pltpu.make_async_copy(own_hbm, own_ref, sem)
    copy.start()
    copy.wait()
    mean, spread = mean_and_spread([own_ref[...].astype(F32), other_ref[...].astype(F32)])
    for i in range(out_ref.shape[0]):
        out_ref[i, 0:1, :] = mean
        out_ref[i, 1:2, :] = spread


def local_stats(own, other, copies):
    vmem = pl.BlockSpec(memory_space=pltpu.VMEM)
    return pl.pallas_call(
        stats_kernel,
        out_shape=(
            jax.ShapeDtypeStruct((copies, 2, own.shape[1]), F32),
            jax.ShapeDtypeStruct(own.shape, own.dtype),
        ),
        in_specs=[pl.BlockSpec(memory_space=pl.ANY), vmem],
        out_specs=(vmem, vmem),
        scratch_shapes=[pltpu.SemaphoreType.DMA],
        cost_estimate=pl.CostEstimate(flops=1 << 20, bytes_accessed=0, transcendentals=0),
        name="local_stats",
    )(own, other)


SPACE_TAPS = (((1, 0),), ((2, 0), (0, 1)))


def prepare_kernel(query_ref, key_ref, value_ref, mix_ref, *refs):
    *vector_refs, qk_ref, vo_ref, vectors_ref, same_ref, member_ref = refs
    width = query_ref.shape[0]
    qk_ref[...] = lax.dot_general(
        query_ref[...], key_ref[...], (((1,), (1,)), ((), ())), preferred_element_type=F32
    ).astype(BF16)
    vo_ref[...] = jnp.dot(value_ref[...], mix_ref[...], preferred_element_type=F32).astype(BF16)
    for i, ref in enumerate(vector_refs):
        vectors_ref[i : i + 1, :] = ref[...].reshape(1, width)
    group = lambda dim: jnp.floor(
        (lax.broadcasted_iota(jnp.int32, (width, width), dim).astype(F32) + 0.5) * (GROUPS / width)
    )
    same_ref[...] = jnp.where(group(0) == group(1), 1.0, 0.0).astype(BF16)
    lane = lax.broadcasted_iota(jnp.int32, member_ref.shape, 1).astype(F32)
    member_ref[...] = jnp.where(group(0)[:, :LANES] == lane, 1.0, 0.0).astype(BF16)


def prepare(query, key, value, mix, *vectors):
    square = jax.ShapeDtypeStruct(query.shape, BF16)
    return pl.pallas_call(
        prepare_kernel,
        out_shape=(
            square,
            square,
            jax.ShapeDtypeStruct((len(vectors), query.shape[0]), F32),
            square,
            jax.ShapeDtypeStruct((query.shape[0], LANES), BF16),
        ),
        cost_estimate=pl.CostEstimate(flops=4 * query.shape[0] ** 3, bytes_accessed=0, transcendentals=0),
        name="prepare",
    )(query, key, value, mix, *vectors)


def merged(stats, count):
    mean = jnp.mean(stats[:, 0], axis=0, keepdims=True)
    gap = stats[:, 0] - mean
    return mean, jnp.sum(stats[:, 1] + gap * gap * count, axis=0, keepdims=True)


def attention_kernel(count, distance_ref, stats_ref, qk_ref, vo_ref, vectors_ref, same_ref, member_ref, *refs):
    *blocks, mixed_ref, out_stats_ref = refs
    positions, width = blocks[0].shape
    cols = positions // 2
    mean, spread = group_mean_and_spread(
        stats_ref[0:1, :], stats_ref[1:2, :], count, same_ref[...]
    )
    variance = exact_product([spread], same_ref[...])[0] * (GROUPS / (width * count))
    gain, shift, bias = (vectors_ref[i : i + 1, :] for i in range(3))
    factor = gain * lax.rsqrt(variance + EPS)
    offset = shift - mean * factor
    scale = width ** (-0.5) * math.log2(math.e)
    below = blocks[1][0:cols, :]
    mask = 3
    while mask < len(blocks):
        below = jnp.where(distance_ref[0] == mask, blocks[mask][0:cols, :], below)
        mask = 2 * mask + 1
    own = jnp.concatenate([blocks[0][...], below], axis=0).astype(F32)
    normed = ((own - mean) * factor + shift).astype(BF16)
    turned = jnp.dot(normed, qk_ref[...], preferred_element_type=F32) * scale
    constant = jnp.sum(turned * offset, axis=1, keepdims=True)
    queries = (turned * factor).astype(BF16)
    highest = None
    for first in range(0, len(blocks), AT_ONCE):
        keys = jnp.concatenate([block[...] for block in blocks[first : first + AT_ONCE]], axis=0)
        scores = lax.dot_general(
            queries, keys, (((1,), (1,)), ((), ())), preferred_element_type=F32
        )
        newest = jnp.max(scores, axis=1, keepdims=True) + constant
        if highest is not None:
            newest = jnp.maximum(highest, newest)
        probs = jnp.exp2(scores + (constant - newest)).astype(BF16)
        wide_keys = jnp.concatenate([keys, jnp.ones((keys.shape[0], 128), BF16)], axis=1)
        product = jnp.dot(probs, wide_keys, preferred_element_type=F32)
        product, part = product[:, :width], product[:, width : width + 1]
        if highest is None:
            total, summed = part, product
        else:
            fade = jnp.exp2(highest - newest)
            total, summed = total * fade + part, summed * fade + product
        highest = newest
    attended = ((summed / total - mean) * factor + shift).astype(BF16)
    branch = jnp.dot(attended, vo_ref[...], preferred_element_type=F32) + bias
    mixed = (own + branch).astype(BF16)
    mixed_ref[...] = mixed
    mean, spread = mean_and_spread([mixed[:positions].astype(F32)])
    _, group_spread = group_mean_and_spread(mean, spread, positions, same_ref[...])
    mean, spread = exact_product([mean * (GROUPS / width), group_spread], member_ref[...])
    for i in range(out_stats_ref.shape[0]):
        out_stats_ref[i, 0:1, :] = mean
        out_stats_ref[i, 1:2, :] = spread


def attention(blocks, distance, stats, count, qk, vo, vectors, same_group, member, stat_copies):
    positions, width = blocks[0].shape
    vmem = pl.BlockSpec(memory_space=pltpu.VMEM)
    return pl.pallas_call(
        functools.partial(attention_kernel, count),
        out_shape=(
            jax.ShapeDtypeStruct((positions // 2 * 3, width), BF16),
            jax.ShapeDtypeStruct((stat_copies, 2, LANES), F32),
        ),
        in_specs=[pl.BlockSpec(memory_space=pltpu.SMEM)] + [vmem] * (6 + len(blocks)),
        out_specs=(vmem, vmem),
        compiler_params=pltpu.CompilerParams(vmem_limit_bytes=VMEM_LIMIT * (2 if len(blocks) > AT_ONCE else 1)),
        name="attention",
    )(distance, stats, qk, vo, vectors, same_group, member, *blocks)


def fetch_kernel(after, weight_hbm, middle_ref, sem):
    copy = pltpu.make_async_copy(weight_hbm.at[:, 1], middle_ref, sem)
    copy.start()
    copy.wait()


def fetch(after, weight):
    width = weight.shape[-1]
    anywhere = pl.BlockSpec(memory_space=pl.ANY)
    return pl.pallas_call(
        fetch_kernel,
        out_shape=pltpu.VMEM((3, 3, width, width), BF16),
        in_specs=[anywhere, anywhere],
        out_specs=pl.BlockSpec(memory_space=pltpu.VMEM),
        scratch_shapes=[pltpu.SemaphoreType.DMA],
        cost_estimate=pl.CostEstimate(flops=0, bytes_accessed=36 * width**2, transcendentals=0),
        compiler_params=pltpu.CompilerParams(vmem_limit_bytes=VMEM_LIMIT),
        name="fetch",
    )(after, pltpu.with_memory_space_constraint(weight, pltpu.HBM))


def upsample_kernel(count, valid_ref, current_ref, earlier_ref, stats_ref, vectors_ref, member_ref, middle_ref, weight_hbm, out_hbm, now, before, wide, out, weight, weight_sems, out_sems):
    positions, width = current_ref.shape
    cols = positions // 3
    copies = {
        r: pltpu.make_async_copy(weight_hbm.at[:, r], weight.at[:, r // 2], weight_sems.at[r // 2]) for r in (2, 0)
    }
    for copy in copies.values():
        copy.start()
    entries = count * width // GROUPS
    mean, spread = merged(stats_ref[...], entries // stats_ref.shape[0])
    mean, variance = exact_product([mean, spread * (1.0 / entries)], member_ref[...], 1)
    gain, shift, bias = (vectors_ref[i : i + 1, :] for i in range(3, 6))
    factor = gain * lax.rsqrt(variance + EPS)
    col = lax.broadcasted_iota(jnp.int32, (cols, width), 0)
    for target, source_ref, known in ((now, current_ref, None), (before, earlier_ref, valid_ref[1])):
        for row in range(3):
            source = source_ref[row * cols : (row + 1) * cols, :]
            value = (source.astype(F32) - mean) * factor + shift
            value = value / (1.0 + jnp.exp(-value))
            kept = known
            if row == 2:
                kept = valid_ref[0] if known is None else valid_ref[0] * known
            if kept is not None:
                value = jnp.where(kept > 0, value, 0.0)
            here = slice(row * cols, (row + 1) * cols)
            target[here, 0:width] = value.astype(BF16)
            moved = jnp.where(col == cols - 1, 0.0, pltpu.roll(value, cols - 1, 0))
            target[here, width : 2 * width] = moved.astype(BF16)
    out_copies = []

    def multiplied(odd_row, odd_col):
        taps = [(r, c) for r, _ in SPACE_TAPS[odd_row] for c, _ in SPACE_TAPS[odd_col]]

        def product(active, *times):
            lanes = slice(0, 2 * width if odd_col else width)
            windows = [active[step * cols : (step + 2) * cols, lanes] for _, step in SPACE_TAPS[odd_row]]
            stacked = [jnp.concatenate([(middle_ref[t, c] if r == 1 else weight[t, r // 2, c]) for t in times], axis=1) for r, c in taps]
            return jnp.dot(
                jnp.concatenate(windows, axis=1),
                jnp.concatenate(stacked, axis=0),
                preferred_element_type=F32,
            )

        both = product(now, 0, 1)
        return both[:, :width] + product(before, 2) + bias, both[:, width:] + bias

    def stored(odd_row, odd_col, sums):
        for odd_time, summed in enumerate(sums):
            for row in range(2):
                for lane in range(width // 128):
                    wide[odd_time, row, lane, pl.ds(odd_col, cols, stride=2), :] = summed[
                        row * cols : (row + 1) * cols, lane * 128 : (lane + 1) * 128
                    ]
                if odd_col == 1:
                    for lane in range(width // 128):
                        out[odd_time, row, odd_row, :, lane * 128 : (lane + 1) * 128] = wide[
                            odd_time, row, lane
                        ].astype(BF16)
            if odd_col == 1:
                place = (odd_time, slice(None), odd_row)
                copy = pltpu.make_async_copy(
                    out.at[*place], out_hbm.at[*place], out_sems.at[odd_time, odd_row]
                )
                copy.start()
                out_copies.append(copy)

    first = [(phase, multiplied(*phase)) for phase in ((0, 0), (0, 1))]
    stored(*first[0][0], first[0][1])
    stored(*first[1][0], first[1][1])
    for copy in copies.values():
        copy.wait()
    for phase in ((1, 0), (1, 1)):
        stored(*phase, multiplied(*phase))
    for copy in out_copies:
        copy.wait()


def upsample(valid, current, earlier, stats, count, vectors, member, middle, weight):
    positions, width = current.shape
    cols = positions // 3
    vmem = pl.BlockSpec(memory_space=pltpu.VMEM)
    result = pl.pallas_call(
        functools.partial(upsample_kernel, count),
        out_shape=jax.ShapeDtypeStruct((2, 2, 2, 2 * cols, width), BF16),
        in_specs=[pl.BlockSpec(memory_space=pltpu.SMEM)]
        + [vmem] * 6
        + [pl.BlockSpec(memory_space=pl.ANY)],
        out_specs=pl.BlockSpec(memory_space=pl.ANY),
        scratch_shapes=[
            pltpu.VMEM((3 * cols, 2 * width), BF16),
            pltpu.VMEM((3 * cols, 2 * width), BF16),
            pltpu.VMEM((2, 2, width // 128, 2 * cols, 128), F32),
            pltpu.VMEM((2, 2, 2, 2 * cols, width), BF16),
            pltpu.VMEM((3, 2, 3, width, width), BF16),
            pltpu.SemaphoreType.DMA((2,)),
            pltpu.SemaphoreType.DMA((2, 2)),
        ],
        compiler_params=pltpu.CompilerParams(vmem_limit_bytes=VMEM_LIMIT),
        name="upsample",
    )(
        valid, current, earlier, stats, vectors, member, middle, pltpu.with_memory_space_constraint(weight, pltpu.HBM)
    )
    return result.reshape(2, 4, 2 * cols, width)


def local(
    latent,
    first_gain,
    first_shift,
    query_weight,
    key_weight,
    value_weight,
    out_weight,
    out_bias,
    second_gain,
    second_shift,
    up_weight,
    up_bias,
):
    frames, rows, cols, width = latent.shape
    positions = rows * cols
    height, groups = lax.axis_size("height"), lax.axis_size("frames")
    slab, group = lax.axis_index("height"), lax.axis_index("frames")
    count = positions * height * groups
    block = latent.reshape(positions, width)

    slots = {0: block, 1: swapped(block, "height", 1)}
    direct = [1 << i for i in range(1, (height - 1).bit_length())]
    forwarded = sorted((m for m in range(2, height, 2) if m not in direct), key=lambda m: (bin(m).count("1"), -m))
    for mask in direct:
        slots[mask] = swapped(block, "height", mask)
    held = 2 * positions

    def early_work(own, other, *parameters):
        stats, own = local_stats(own, other, groups)
        stats = lax.all_to_all(stats, "frames", split_axis=0, concat_axis=0, tiled=True)
        return jnp.concatenate(merged(stats, held), axis=0), own, *prepare(*parameters)

    parameters = (query_weight, key_weight, value_weight, out_weight)
    parameters += (first_gain, first_shift, out_bias, second_gain, second_shift, up_bias)
    first, slots[0], qk, vo, vectors, same_group, member = lax.cond(
        group < groups,
        early_work,
        lambda *arguments: jax.tree.map(
            lambda kind: jnp.zeros(kind.shape, kind.dtype), jax.eval_shape(early_work, *arguments)
        ),
        block,
        slots[1],
        *parameters,
    )
    held = held * groups
    _, *ready = lax.optimization_barrier([first] + [slots[m] for m in direct])
    slots.update(zip(direct, ready))
    for mask in forwarded:
        lowest = mask & -mask
        slots[mask] = swapped(slots[mask ^ lowest], "height", lowest)
    for mask in direct:
        pair = jnp.stack([first, swapped(first, "height", mask)])
        first, held = jnp.concatenate(merged(pair, held), axis=0), held * 2
    for mask in direct + forwarded:
        slots[mask | 1] = swapped(slots[mask], "height", 1)
    distance = (slab ^ (slab + 1)).astype(jnp.int32).reshape(1)

    blocks = [slots[m] for m in range(height)]
    mixed, second = attention(
        blocks, distance, first, count, qk, vo, vectors, same_group, member, groups * height
    )
    middle = fetch(mixed, up_weight)
    earlier = lax.ppermute(mixed, "frames", [(i, (i + 1) % groups) for i in range(groups)])
    second = lax.all_to_all(second, ("frames", "height"), split_axis=0, concat_axis=0, tiled=True)
    valid = jnp.stack([slab + 1 < height, group > 0]).astype(jnp.int32)
    return upsample(
        valid, mixed, earlier, second, count, vectors, member, middle, up_weight
    )


def solution(mesh):
    placed = P("frames", "height", None, None)
    return jax.shard_map(
        local,
        mesh=mesh,
        in_specs=(placed,) + (P(),) * 11,
        out_specs=placed,
        check_vma=False,
    )
```

```python
import functools
import math

import jax
import jax.numpy as jnp
import numpy as np
from jax import lax
from jax.experimental import pallas as pl
from jax.experimental.pallas import tpu as pltpu
from jax.sharding import PartitionSpec as P

GROUPS = 32
EPS = 1e-05
F32 = jnp.float32
BF16 = jnp.bfloat16
VMEM_LIMIT = 26 * 1024 * 1024
AT_ONCE = 8
LANES = 128


def swapped(value, axis, mask):
    count = lax.axis_size(axis)
    return lax.ppermute(value, axis, [(i, i ^ mask) for i in range(count)])


def exact_product(rows, matrix, contracted=0):
    row = lax.broadcasted_iota(jnp.int32, (8 * len(rows), rows[0].shape[1]), 0)
    parts = jnp.zeros(row.shape, F32)
    for i, rest in enumerate(rows):
        for j in range(3):
            part = rest.astype(BF16).astype(F32)
            rest = rest - part
            parts = jnp.where(row == 8 * i + j, part, parts)
    summed = lax.dot_general(
        parts.astype(BF16), matrix, (((1,), (contracted,)), ((), ())), preferred_element_type=F32
    )
    return [jnp.sum(summed[8 * i : 8 * i + 8], axis=0, keepdims=True) for i in range(len(rows))]


def mean_and_spread(blocks):
    count = len(blocks) * blocks[0].shape[0]
    mean = sum(jnp.sum(b, axis=0, keepdims=True) for b in blocks) * (1.0 / count)
    return mean, sum(jnp.sum(jnp.square(b - mean), axis=0, keepdims=True) for b in blocks)


def group_mean_and_spread(means, spread, count, same_group):
    mean = exact_product([means], same_group)[0] * (GROUPS / means.shape[1])
    gap = means - mean
    return mean, spread + gap * gap * count


def stats_kernel(own_hbm, other_ref, out_ref, own_ref, sem):
    copy = pltpu.make_async_copy(own_hbm, own_ref, sem)
    copy.start()
    copy.wait()
    mean, spread = mean_and_spread([own_ref[...].astype(F32), other_ref[...].astype(F32)])
    for i in range(out_ref.shape[0]):
        out_ref[i, 0:1, :] = mean
        out_ref[i, 1:2, :] = spread


def local_stats(own, other, copies):
    vmem = pl.BlockSpec(memory_space=pltpu.VMEM)
    return pl.pallas_call(
        stats_kernel,
        out_shape=(
            jax.ShapeDtypeStruct((copies, 2, own.shape[1]), F32),
            jax.ShapeDtypeStruct(own.shape, own.dtype),
        ),
        in_specs=[pl.BlockSpec(memory_space=pl.ANY), vmem],
        out_specs=(vmem, vmem),
        scratch_shapes=[pltpu.SemaphoreType.DMA],
        cost_estimate=pl.CostEstimate(flops=1 << 20, bytes_accessed=0, transcendentals=0),
        name="local_stats",
    )(own, other)


SPACE_TAPS = (((1, 0),), ((2, 0), (0, 1)))


def prepare_kernel(query_ref, key_ref, value_ref, mix_ref, *refs):
    *vector_refs, qk_ref, vo_ref, vectors_ref, same_ref, member_ref = refs
    width = query_ref.shape[0]
    qk_ref[...] = lax.dot_general(
        query_ref[...], key_ref[...], (((1,), (1,)), ((), ())), preferred_element_type=F32
    ).astype(BF16)
    vo_ref[...] = jnp.dot(value_ref[...], mix_ref[...], preferred_element_type=F32).astype(BF16)
    for i, ref in enumerate(vector_refs):
        vectors_ref[i : i + 1, :] = ref[...].reshape(1, width)
    group = lambda dim: jnp.floor(
        (lax.broadcasted_iota(jnp.int32, (width, width), dim).astype(F32) + 0.5) * (GROUPS / width)
    )
    same_ref[...] = jnp.where(group(0) == group(1), 1.0, 0.0).astype(BF16)
    lane = lax.broadcasted_iota(jnp.int32, member_ref.shape, 1).astype(F32)
    member_ref[...] = jnp.where(group(0)[:, :LANES] == lane, 1.0, 0.0).astype(BF16)


def prepare(query, key, value, mix, *vectors):
    square = jax.ShapeDtypeStruct(query.shape, BF16)
    return pl.pallas_call(
        prepare_kernel,
        out_shape=(
            square,
            square,
            jax.ShapeDtypeStruct((len(vectors), query.shape[0]), F32),
            square,
            jax.ShapeDtypeStruct((query.shape[0], LANES), BF16),
        ),
        cost_estimate=pl.CostEstimate(flops=4 * query.shape[0] ** 3, bytes_accessed=0, transcendentals=0),
        name="prepare",
    )(query, key, value, mix, *vectors)


def merged(stats, count):
    mean = jnp.mean(stats[:, 0], axis=0, keepdims=True)
    gap = stats[:, 0] - mean
    return mean, jnp.sum(stats[:, 1] + gap * gap * count, axis=0, keepdims=True)


def attention_kernel(count, distance_ref, stats_ref, qk_ref, vo_ref, vectors_ref, same_ref, member_ref, *refs):
    *blocks, mixed_ref, out_stats_ref = refs
    positions, width = blocks[0].shape
    cols = positions // 2
    mean, spread = group_mean_and_spread(
        stats_ref[0:1, :], stats_ref[1:2, :], count, same_ref[...]
    )
    variance = exact_product([spread], same_ref[...])[0] * (GROUPS / (width * count))
    gain, shift, bias = (vectors_ref[i : i + 1, :] for i in range(3))
    factor = gain * lax.rsqrt(variance + EPS)
    offset = shift - mean * factor
    scale = width ** (-0.5) * math.log2(math.e)
    below = blocks[1][0:cols, :]
    mask = 3
    while mask < len(blocks):
        below = jnp.where(distance_ref[0] == mask, blocks[mask][0:cols, :], below)
        mask = 2 * mask + 1
    own = jnp.concatenate([blocks[0][...], below], axis=0).astype(F32)
    normed = ((own - mean) * factor + shift).astype(BF16)
    turned = jnp.dot(normed, qk_ref[...], preferred_element_type=F32) * scale
    constant = jnp.sum(turned * offset, axis=1, keepdims=True)
    queries = (turned * factor).astype(BF16)
    highest = None
    for first in range(0, len(blocks), AT_ONCE):
        keys = jnp.concatenate([block[...] for block in blocks[first : first + AT_ONCE]], axis=0)
        scores = lax.dot_general(
            queries, keys, (((1,), (1,)), ((), ())), preferred_element_type=F32
        )
        newest = jnp.max(scores, axis=1, keepdims=True) + constant
        if highest is not None:
            newest = jnp.maximum(highest, newest)
        probs = jnp.exp2(scores + (constant - newest)).astype(BF16)
        wide_keys = jnp.concatenate([keys, jnp.ones((keys.shape[0], 128), BF16)], axis=1)
        product = jnp.dot(probs, wide_keys, preferred_element_type=F32)
        product, part = product[:, :width], product[:, width : width + 1]
        if highest is None:
            total, summed = part, product
        else:
            fade = jnp.exp2(highest - newest)
            total, summed = total * fade + part, summed * fade + product
        highest = newest
    attended = ((summed / total - mean) * factor + shift).astype(BF16)
    branch = jnp.dot(attended, vo_ref[...], preferred_element_type=F32) + bias
    mixed = (own + branch).astype(BF16)
    mixed_ref[...] = mixed
    mean, spread = mean_and_spread([mixed[:positions].astype(F32)])
    _, group_spread = group_mean_and_spread(mean, spread, positions, same_ref[...])
    mean, spread = exact_product([mean * (GROUPS / width), group_spread], member_ref[...])
    for i in range(out_stats_ref.shape[0]):
        out_stats_ref[i, 0:1, :] = mean
        out_stats_ref[i, 1:2, :] = spread


def attention(blocks, distance, stats, count, qk, vo, vectors, same_group, member, stat_copies):
    positions, width = blocks[0].shape
    vmem = pl.BlockSpec(memory_space=pltpu.VMEM)
    return pl.pallas_call(
        functools.partial(attention_kernel, count),
        out_shape=(
            jax.ShapeDtypeStruct((positions // 2 * 3, width), BF16),
            jax.ShapeDtypeStruct((stat_copies, 2, LANES), F32),
        ),
        in_specs=[pl.BlockSpec(memory_space=pltpu.SMEM)] + [vmem] * (6 + len(blocks)),
        out_specs=(vmem, vmem),
        compiler_params=pltpu.CompilerParams(vmem_limit_bytes=VMEM_LIMIT * (2 if len(blocks) > AT_ONCE else 1)),
        name="attention",
    )(distance, stats, qk, vo, vectors, same_group, member, *blocks)


def fetch_kernel(after, weight_hbm, middle_ref, sem):
    copy = pltpu.make_async_copy(weight_hbm.at[:, 1], middle_ref, sem)
    copy.start()
    copy.wait()


def fetch(after, weight):
    width = weight.shape[-1]
    anywhere = pl.BlockSpec(memory_space=pl.ANY)
    return pl.pallas_call(
        fetch_kernel,
        out_shape=pltpu.VMEM((3, 3, width, width), BF16),
        in_specs=[anywhere, anywhere],
        out_specs=pl.BlockSpec(memory_space=pltpu.VMEM),
        scratch_shapes=[pltpu.SemaphoreType.DMA],
        cost_estimate=pl.CostEstimate(flops=0, bytes_accessed=36 * width**2, transcendentals=0),
        compiler_params=pltpu.CompilerParams(vmem_limit_bytes=VMEM_LIMIT),
        name="fetch",
    )(after, pltpu.with_memory_space_constraint(weight, pltpu.HBM))


def upsample_kernel(count, valid_ref, current_ref, earlier_ref, stats_ref, vectors_ref, member_ref, middle_ref, weight_hbm, out_hbm, now, before, wide, out, weight, weight_sems, out_sems):
    positions, width = current_ref.shape
    cols = positions // 3
    copies = {
        r: pltpu.make_async_copy(weight_hbm.at[:, r], weight.at[:, r // 2], weight_sems.at[r // 2]) for r in (2, 0)
    }
    for copy in copies.values():
        copy.start()
    entries = count * width // GROUPS
    mean, spread = merged(stats_ref[...], entries // stats_ref.shape[0])
    mean, variance = exact_product([mean, spread * (1.0 / entries)], member_ref[...], 1)
    gain, shift, bias = (vectors_ref[i : i + 1, :] for i in range(3, 6))
    factor = gain * lax.rsqrt(variance + EPS)
    col = lax.broadcasted_iota(jnp.int32, (cols, width), 0)
    for target, source_ref, known in ((now, current_ref, None), (before, earlier_ref, valid_ref[1])):
        for row in range(3):
            source = source_ref[row * cols : (row + 1) * cols, :]
            value = (source.astype(F32) - mean) * factor + shift
            value = value / (1.0 + jnp.exp(-value))
            kept = known
            if row == 2:
                kept = valid_ref[0] if known is None else valid_ref[0] * known
            if kept is not None:
                value = jnp.where(kept > 0, value, 0.0)
            here = slice(row * cols, (row + 1) * cols)
            target[here, 0:width] = value.astype(BF16)
            moved = jnp.where(col == cols - 1, 0.0, pltpu.roll(value, cols - 1, 0))
            target[here, width : 2 * width] = moved.astype(BF16)
    out_copies = []

    def multiplied(odd_row, odd_col):
        taps = [(r, c) for r, _ in SPACE_TAPS[odd_row] for c, _ in SPACE_TAPS[odd_col]]

        def product(active, *times):
            lanes = slice(0, 2 * width if odd_col else width)
            windows = [active[step * cols : (step + 2) * cols, lanes] for _, step in SPACE_TAPS[odd_row]]
            stacked = [jnp.concatenate([(middle_ref[t, c] if r == 1 else weight[t, r // 2, c]) for t in times], axis=1) for r, c in taps]
            return jnp.dot(
                jnp.concatenate(windows, axis=1),
                jnp.concatenate(stacked, axis=0),
                preferred_element_type=F32,
            )

        both = product(now, 0, 1)
        return both[:, :width] + product(before, 2) + bias, both[:, width:] + bias

    def stored(odd_row, odd_col, sums):
        for odd_time, summed in enumerate(sums):
            for row in range(2):
                for lane in range(width // 128):
                    wide[odd_time, row, lane, pl.ds(odd_col, cols, stride=2), :] = summed[
                        row * cols : (row + 1) * cols, lane * 128 : (lane + 1) * 128
                    ]
                if odd_col == 1:
                    for lane in range(width // 128):
                        out[odd_time, row, odd_row, :, lane * 128 : (lane + 1) * 128] = wide[
                            odd_time, row, lane
                        ].astype(BF16)
            if odd_col == 1:
                place = (odd_time, slice(None), odd_row)
                copy = pltpu.make_async_copy(
                    out.at[*place], out_hbm.at[*place], out_sems.at[odd_time, odd_row]
                )
                copy.start()
                out_copies.append(copy)

    first = [(phase, multiplied(*phase)) for phase in ((0, 0), (0, 1))]
    stored(*first[0][0], first[0][1])
    stored(*first[1][0], first[1][1])
    for copy in copies.values():
        copy.wait()
    for phase in ((1, 0), (1, 1)):
        stored(*phase, multiplied(*phase))
    for copy in out_copies:
        copy.wait()


def upsample(valid, current, earlier, stats, count, vectors, member, middle, weight):
    positions, width = current.shape
    cols = positions // 3
    vmem = pl.BlockSpec(memory_space=pltpu.VMEM)
    result = pl.pallas_call(
        functools.partial(upsample_kernel, count),
        out_shape=jax.ShapeDtypeStruct((2, 2, 2, 2 * cols, width), BF16),
        in_specs=[pl.BlockSpec(memory_space=pltpu.SMEM)]
        + [vmem] * 6
        + [pl.BlockSpec(memory_space=pl.ANY)],
        out_specs=pl.BlockSpec(memory_space=pl.ANY),
        scratch_shapes=[
            pltpu.VMEM((3 * cols, 2 * width), BF16),
            pltpu.VMEM((3 * cols, 2 * width), BF16),
            pltpu.VMEM((2, 2, width // 128, 2 * cols, 128), F32),
            pltpu.VMEM((2, 2, 2, 2 * cols, width), BF16),
            pltpu.VMEM((3, 2, 3, width, width), BF16),
            pltpu.SemaphoreType.DMA((2,)),
            pltpu.SemaphoreType.DMA((2, 2)),
        ],
        compiler_params=pltpu.CompilerParams(vmem_limit_bytes=VMEM_LIMIT),
        name="upsample",
    )(
        valid, current, earlier, stats, vectors, member, middle, pltpu.with_memory_space_constraint(weight, pltpu.HBM)
    )
    return result.reshape(2, 4, 2 * cols, width)


def local(
    latent,
    first_gain,
    first_shift,
    query_weight,
    key_weight,
    value_weight,
    out_weight,
    out_bias,
    second_gain,
    second_shift,
    up_weight,
    up_bias,
):
    frames, rows, cols, width = latent.shape
    positions = rows * cols
    height, groups = lax.axis_size("height"), lax.axis_size("frames")
    slab, group = lax.axis_index("height"), lax.axis_index("frames")
    count = positions * height * groups
    block = latent.reshape(positions, width)

    slots = {0: block, 1: swapped(block, "height", 1)}
    direct = [1 << i for i in range(1, (height - 1).bit_length())][::-1]
    forwarded = sorted((m for m in range(2, height, 2) if m not in direct), key=lambda m: (bin(m).count("1"), -m))
    for mask in direct:
        slots[mask] = swapped(block, "height", mask)
    held = 2 * positions

    def early_work(own, other, *parameters):
        stats, own = local_stats(own, other, 1)
        masks = range(1, groups)
        stats = jnp.stack([stats[0]] + [swapped(stats[0], "frames", mask) for mask in masks])
        return jnp.concatenate(merged(stats, held), axis=0), own, *prepare(*parameters)

    parameters = (query_weight, key_weight, value_weight, out_weight)
    parameters += (first_gain, first_shift, out_bias, second_gain, second_shift, up_bias)
    first, slots[0], qk, vo, vectors, same_group, member = lax.cond(
        group < groups,
        early_work,
        lambda *arguments: jax.tree.map(
            lambda kind: jnp.zeros(kind.shape, kind.dtype), jax.eval_shape(early_work, *arguments)
        ),
        block,
        slots[1],
        *parameters,
    )
    held = held * groups
    _, *ready = lax.optimization_barrier([first] + [slots[m] for m in direct])
    slots.update(zip(direct, ready))
    for mask in forwarded:
        lowest = mask & -mask
        slots[mask] = swapped(slots[mask ^ lowest], "height", lowest)
    for mask in direct:
        pair = jnp.stack([first, swapped(first, "height", mask)])
        first, held = jnp.concatenate(merged(pair, held), axis=0), held * 2
    for mask in direct + forwarded:
        slots[mask | 1] = swapped(slots[mask], "height", 1)
    distance = (slab ^ (slab + 1)).astype(jnp.int32).reshape(1)

    blocks = [slots[m] for m in range(height)]
    mixed, second = attention(
        blocks, distance, first, count, qk, vo, vectors, same_group, member, groups * height
    )
    middle = fetch(mixed, up_weight)
    earlier = lax.ppermute(mixed, "frames", [(i, (i + 1) % groups) for i in range(groups)])
    second = lax.all_to_all(second, ("frames", "height"), split_axis=0, concat_axis=0, tiled=True)
    valid = jnp.stack([slab + 1 < height, group > 0]).astype(jnp.int32)
    return upsample(
        valid, mixed, earlier, second, count, vectors, member, middle, up_weight
    )


def solution(mesh):
    placed = P("frames", "height", None, None)
    return jax.shard_map(
        local,
        mesh=mesh,
        in_specs=(placed,) + (P(),) * 11,
        out_specs=placed,
        check_vma=False,
    )
```

```python
import functools
import math

import jax
import jax.numpy as jnp
import numpy as np
from jax import lax
from jax.experimental import pallas as pl
from jax.experimental.pallas import tpu as pltpu
from jax.sharding import PartitionSpec as P

GROUPS = 32
EPS = 1e-05
F32 = jnp.float32
BF16 = jnp.bfloat16
VMEM_LIMIT = 26 * 1024 * 1024
AT_ONCE = 8
LANES = 128


def swapped(value, axis, mask):
    count = lax.axis_size(axis)
    return lax.ppermute(value, axis, [(i, i ^ mask) for i in range(count)])


def exact_product(rows, matrix, contracted=0):
    row = lax.broadcasted_iota(jnp.int32, (8 * len(rows), rows[0].shape[1]), 0)
    parts = jnp.zeros(row.shape, F32)
    for i, rest in enumerate(rows):
        for j in range(3):
            part = rest.astype(BF16).astype(F32)
            rest = rest - part
            parts = jnp.where(row == 8 * i + j, part, parts)
    summed = lax.dot_general(
        parts.astype(BF16), matrix, (((1,), (contracted,)), ((), ())), preferred_element_type=F32
    )
    return [jnp.sum(summed[8 * i : 8 * i + 8], axis=0, keepdims=True) for i in range(len(rows))]


def mean_and_spread(blocks):
    count = len(blocks) * blocks[0].shape[0]
    mean = sum(jnp.sum(b, axis=0, keepdims=True) for b in blocks) * (1.0 / count)
    return mean, sum(jnp.sum(jnp.square(b - mean), axis=0, keepdims=True) for b in blocks)


def group_mean_and_spread(means, spread, count, same_group):
    mean = exact_product([means], same_group)[0] * (GROUPS / means.shape[1])
    gap = means - mean
    return mean, spread + gap * gap * count


def stats_kernel(own_hbm, other_ref, out_ref, own_ref, sem):
    copy = pltpu.make_async_copy(own_hbm, own_ref, sem)
    copy.start()
    copy.wait()
    mean, spread = mean_and_spread([own_ref[...].astype(F32), other_ref[...].astype(F32)])
    for i in range(out_ref.shape[0]):
        out_ref[i, 0:1, :] = mean
        out_ref[i, 1:2, :] = spread


def local_stats(own, other, copies):
    vmem = pl.BlockSpec(memory_space=pltpu.VMEM)
    return pl.pallas_call(
        stats_kernel,
        out_shape=(
            jax.ShapeDtypeStruct((copies, 2, own.shape[1]), F32),
            jax.ShapeDtypeStruct(own.shape, own.dtype),
        ),
        in_specs=[pl.BlockSpec(memory_space=pl.ANY), vmem],
        out_specs=(vmem, vmem),
        scratch_shapes=[pltpu.SemaphoreType.DMA],
        cost_estimate=pl.CostEstimate(flops=1 << 20, bytes_accessed=0, transcendentals=0),
        name="local_stats",
    )(own, other)


SPACE_TAPS = (((1, 0),), ((2, 0), (0, 1)))


def prepare_kernel(query_ref, key_ref, value_ref, mix_ref, *refs):
    *vector_refs, qk_ref, vo_ref, vectors_ref, same_ref, member_ref = refs
    width = query_ref.shape[0]
    qk_ref[...] = lax.dot_general(
        query_ref[...], key_ref[...], (((1,), (1,)), ((), ())), preferred_element_type=F32
    ).astype(BF16)
    vo_ref[...] = jnp.dot(value_ref[...], mix_ref[...], preferred_element_type=F32).astype(BF16)
    for i, ref in enumerate(vector_refs):
        vectors_ref[i : i + 1, :] = ref[...].reshape(1, width)
    group = lambda dim: jnp.floor(
        (lax.broadcasted_iota(jnp.int32, (width, width), dim).astype(F32) + 0.5) * (GROUPS / width)
    )
    same_ref[...] = jnp.where(group(0) == group(1), 1.0, 0.0).astype(BF16)
    lane = lax.broadcasted_iota(jnp.int32, member_ref.shape, 1).astype(F32)
    member_ref[...] = jnp.where(group(0)[:, :LANES] == lane, 1.0, 0.0).astype(BF16)


def prepare(query, key, value, mix, *vectors):
    square = jax.ShapeDtypeStruct(query.shape, BF16)
    return pl.pallas_call(
        prepare_kernel,
        out_shape=(
            square,
            square,
            jax.ShapeDtypeStruct((len(vectors), query.shape[0]), F32),
            square,
            jax.ShapeDtypeStruct((query.shape[0], LANES), BF16),
        ),
        cost_estimate=pl.CostEstimate(flops=4 * query.shape[0] ** 3, bytes_accessed=0, transcendentals=0),
        name="prepare",
    )(query, key, value, mix, *vectors)


def merged(stats, count):
    mean = jnp.mean(stats[:, 0], axis=0, keepdims=True)
    gap = stats[:, 0] - mean
    return mean, jnp.sum(stats[:, 1] + gap * gap * count, axis=0, keepdims=True)


def attention_kernel(count, distance_ref, stats_ref, qk_ref, vo_ref, vectors_ref, same_ref, member_ref, *refs):
    *blocks, mixed_ref, out_stats_ref = refs
    positions, width = blocks[0].shape
    cols = positions // 2
    mean, spread = group_mean_and_spread(
        stats_ref[0:1, :], stats_ref[1:2, :], count, same_ref[...]
    )
    variance = exact_product([spread], same_ref[...])[0] * (GROUPS / (width * count))
    gain, shift, bias = (vectors_ref[i : i + 1, :] for i in range(3))
    factor = gain * lax.rsqrt(variance + EPS)
    offset = shift - mean * factor
    scale = width ** (-0.5) * math.log2(math.e)
    below = blocks[1][0:cols, :]
    mask = 3
    while mask < len(blocks):
        below = jnp.where(distance_ref[0] == mask, blocks[mask][0:cols, :], below)
        mask = 2 * mask + 1
    own = jnp.concatenate([blocks[0][...], below], axis=0).astype(F32)
    normed = ((own - mean) * factor + shift).astype(BF16)
    turned = jnp.dot(normed, qk_ref[...], preferred_element_type=F32) * scale
    constant = jnp.sum(turned * offset, axis=1, keepdims=True)
    queries = (turned * factor).astype(BF16)
    highest = None
    for first in range(0, len(blocks), AT_ONCE):
        keys = jnp.concatenate([block[...] for block in blocks[first : first + AT_ONCE]], axis=0)
        scores = lax.dot_general(
            queries, keys, (((1,), (1,)), ((), ())), preferred_element_type=F32
        )
        newest = jnp.max(scores, axis=1, keepdims=True) + constant
        if highest is not None:
            newest = jnp.maximum(highest, newest)
        probs = jnp.exp2(scores + (constant - newest)).astype(BF16)
        wide_keys = jnp.concatenate([keys, jnp.ones((keys.shape[0], 128), BF16)], axis=1)
        product = jnp.dot(probs, wide_keys, preferred_element_type=F32)
        product, part = product[:, :width], product[:, width : width + 1]
        if highest is None:
            total, summed = part, product
        else:
            fade = jnp.exp2(highest - newest)
            total, summed = total * fade + part, summed * fade + product
        highest = newest
    attended = ((summed / total - mean) * factor + shift).astype(BF16)
    branch = jnp.dot(attended, vo_ref[...], preferred_element_type=F32) + bias
    mixed = (own + branch).astype(BF16)
    mixed_ref[...] = mixed
    mean, spread = mean_and_spread([mixed[:positions].astype(F32)])
    _, group_spread = group_mean_and_spread(mean, spread, positions, same_ref[...])
    mean, spread = exact_product([mean * (GROUPS / width), group_spread], member_ref[...])
    for i in range(out_stats_ref.shape[0]):
        out_stats_ref[i, 0:1, :] = mean
        out_stats_ref[i, 1:2, :] = spread


def attention(blocks, distance, stats, count, qk, vo, vectors, same_group, member, stat_copies):
    positions, width = blocks[0].shape
    vmem = pl.BlockSpec(memory_space=pltpu.VMEM)
    return pl.pallas_call(
        functools.partial(attention_kernel, count),
        out_shape=(
            jax.ShapeDtypeStruct((positions // 2 * 3, width), BF16),
            jax.ShapeDtypeStruct((stat_copies, 2, LANES), F32),
        ),
        in_specs=[pl.BlockSpec(memory_space=pltpu.SMEM)] + [vmem] * (6 + len(blocks)),
        out_specs=(vmem, vmem),
        compiler_params=pltpu.CompilerParams(vmem_limit_bytes=VMEM_LIMIT * (2 if len(blocks) > AT_ONCE else 1)),
        name="attention",
    )(distance, stats, qk, vo, vectors, same_group, member, *blocks)


def fetch_kernel(after, weight_hbm, middle_ref, sem):
    copy = pltpu.make_async_copy(weight_hbm.at[:, 1], middle_ref, sem)
    copy.start()
    copy.wait()


def fetch(after, weight):
    width = weight.shape[-1]
    anywhere = pl.BlockSpec(memory_space=pl.ANY)
    return pl.pallas_call(
        fetch_kernel,
        out_shape=pltpu.VMEM((3, 3, width, width), BF16),
        in_specs=[anywhere, anywhere],
        out_specs=pl.BlockSpec(memory_space=pltpu.VMEM),
        scratch_shapes=[pltpu.SemaphoreType.DMA],
        cost_estimate=pl.CostEstimate(flops=0, bytes_accessed=36 * width**2, transcendentals=0),
        compiler_params=pltpu.CompilerParams(vmem_limit_bytes=VMEM_LIMIT),
        name="fetch",
    )(after, pltpu.with_memory_space_constraint(weight, pltpu.HBM))


def upsample_kernel(count, valid_ref, current_ref, earlier_ref, stats_ref, vectors_ref, member_ref, middle_ref, weight_hbm, out_hbm, now, before, wide, out, weight, weight_sems, out_sems):
    positions, width = current_ref.shape
    cols = positions // 3
    copies = {
        r: pltpu.make_async_copy(weight_hbm.at[:, r], weight.at[:, r // 2], weight_sems.at[r // 2]) for r in (2, 0)
    }
    for copy in copies.values():
        copy.start()
    entries = count * width // GROUPS
    mean, spread = merged(stats_ref[...], entries // stats_ref.shape[0])
    mean, variance = exact_product([mean, spread * (1.0 / entries)], member_ref[...], 1)
    gain, shift, bias = (vectors_ref[i : i + 1, :] for i in range(3, 6))
    factor = gain * lax.rsqrt(variance + EPS)
    col = lax.broadcasted_iota(jnp.int32, (cols, width), 0)
    for target, source_ref, known in ((now, current_ref, None), (before, earlier_ref, valid_ref[1])):
        for row in range(3):
            source = source_ref[row * cols : (row + 1) * cols, :]
            value = (source.astype(F32) - mean) * factor + shift
            value = value / (1.0 + jnp.exp(-value))
            kept = known
            if row == 2:
                kept = valid_ref[0] if known is None else valid_ref[0] * known
            if kept is not None:
                value = jnp.where(kept > 0, value, 0.0)
            here = slice(row * cols, (row + 1) * cols)
            target[here, 0:width] = value.astype(BF16)
            moved = jnp.where(col == cols - 1, 0.0, pltpu.roll(value, cols - 1, 0))
            target[here, width : 2 * width] = moved.astype(BF16)
    out_copies = []

    def multiplied(odd_row, odd_col):
        taps = [(r, c) for r, _ in SPACE_TAPS[odd_row] for c, _ in SPACE_TAPS[odd_col]]

        def product(active, *times):
            lanes = slice(0, 2 * width if odd_col else width)
            windows = [active[step * cols : (step + 2) * cols, lanes] for _, step in SPACE_TAPS[odd_row]]
            stacked = [jnp.concatenate([(middle_ref[t, c] if r == 1 else weight[t, r // 2, c]) for t in times], axis=1) for r, c in taps]
            return jnp.dot(
                jnp.concatenate(windows, axis=1),
                jnp.concatenate(stacked, axis=0),
                preferred_element_type=F32,
            )

        both = product(now, 0, 1)
        return both[:, :width] + product(before, 2) + bias, both[:, width:] + bias

    def stored(odd_row, odd_col, sums):
        for odd_time, summed in enumerate(sums):
            for row in range(2):
                for lane in range(width // 128):
                    wide[odd_time, row, lane, pl.ds(odd_col, cols, stride=2), :] = summed[
                        row * cols : (row + 1) * cols, lane * 128 : (lane + 1) * 128
                    ]
                if odd_col == 1:
                    for lane in range(width // 128):
                        out[odd_time, row, odd_row, :, lane * 128 : (lane + 1) * 128] = wide[
                            odd_time, row, lane
                        ].astype(BF16)
                    place = (odd_time, row, odd_row)
                    copy = pltpu.make_async_copy(out.at[*place], out_hbm.at[*place], out_sems.at[*place])
                    copy.start()
                    out_copies.append(copy)

    first = [(phase, multiplied(*phase)) for phase in ((0, 0), (0, 1))]
    stored(*first[0][0], first[0][1])
    stored(*first[1][0], first[1][1])
    for copy in copies.values():
        copy.wait()
    for phase in ((1, 0), (1, 1)):
        stored(*phase, multiplied(*phase))
    for copy in out_copies:
        copy.wait()


def upsample(valid, current, earlier, stats, count, vectors, member, middle, weight):
    positions, width = current.shape
    cols = positions // 3
    vmem = pl.BlockSpec(memory_space=pltpu.VMEM)
    result = pl.pallas_call(
        functools.partial(upsample_kernel, count),
        out_shape=jax.ShapeDtypeStruct((2, 2, 2, 2 * cols, width), BF16),
        in_specs=[pl.BlockSpec(memory_space=pltpu.SMEM)]
        + [vmem] * 6
        + [pl.BlockSpec(memory_space=pl.ANY)],
        out_specs=pl.BlockSpec(memory_space=pl.ANY),
        scratch_shapes=[
            pltpu.VMEM((3 * cols, 2 * width), BF16),
            pltpu.VMEM((3 * cols, 2 * width), BF16),
            pltpu.VMEM((2, 2, width // 128, 2 * cols, 128), F32),
            pltpu.VMEM((2, 2, 2, 2 * cols, width), BF16),
            pltpu.VMEM((3, 2, 3, width, width), BF16),
            pltpu.SemaphoreType.DMA((2,)),
            pltpu.SemaphoreType.DMA((2, 2, 2)),
        ],
        compiler_params=pltpu.CompilerParams(vmem_limit_bytes=VMEM_LIMIT),
        name="upsample",
    )(
        valid, current, earlier, stats, vectors, member, middle, pltpu.with_memory_space_constraint(weight, pltpu.HBM)
    )
    return result.reshape(2, 4, 2 * cols, width)


def local(
    latent,
    first_gain,
    first_shift,
    query_weight,
    key_weight,
    value_weight,
    out_weight,
    out_bias,
    second_gain,
    second_shift,
    up_weight,
    up_bias,
):
    frames, rows, cols, width = latent.shape
    positions = rows * cols
    height, groups = lax.axis_size("height"), lax.axis_size("frames")
    slab, group = lax.axis_index("height"), lax.axis_index("frames")
    count = positions * height * groups
    block = latent.reshape(positions, width)

    slots = {0: block, 1: swapped(block, "height", 1)}
    direct = [1 << i for i in range(1, (height - 1).bit_length())][::-1]
    forwarded = sorted((m for m in range(2, height, 2) if m not in direct), key=lambda m: (bin(m).count("1"), -m))
    for mask in direct:
        slots[mask] = swapped(block, "height", mask)
    held = 2 * positions

    def early_work(own, other, *parameters):
        stats, own = local_stats(own, other, 1)
        masks = range(1, groups)
        stats = jnp.stack([stats[0]] + [swapped(stats[0], "frames", mask) for mask in masks])
        return jnp.concatenate(merged(stats, held), axis=0), own, *prepare(*parameters)

    parameters = (query_weight, key_weight, value_weight, out_weight)
    parameters += (first_gain, first_shift, out_bias, second_gain, second_shift, up_bias)
    first, slots[0], qk, vo, vectors, same_group, member = lax.cond(
        group < groups,
        early_work,
        lambda *arguments: jax.tree.map(
            lambda kind: jnp.zeros(kind.shape, kind.dtype), jax.eval_shape(early_work, *arguments)
        ),
        block,
        slots[1],
        *parameters,
    )
    held = held * groups
    _, *ready = lax.optimization_barrier([first] + [slots[m] for m in direct])
    slots.update(zip(direct, ready))
    for mask in forwarded:
        lowest = mask & -mask
        slots[mask] = swapped(slots[mask ^ lowest], "height", lowest)
    for mask in direct:
        pair = jnp.stack([first, swapped(first, "height", mask)])
        first, held = jnp.concatenate(merged(pair, held), axis=0), held * 2
    for mask in direct + forwarded:
        slots[mask | 1] = swapped(slots[mask], "height", 1)
    distance = (slab ^ (slab + 1)).astype(jnp.int32).reshape(1)

    blocks = [slots[m] for m in range(height)]
    mixed, second = attention(
        blocks, distance, first, count, qk, vo, vectors, same_group, member, groups * height
    )
    middle = fetch(mixed, up_weight)
    earlier = lax.ppermute(mixed, "frames", [(i, (i + 1) % groups) for i in range(groups)])
    second = lax.all_to_all(second, ("frames", "height"), split_axis=0, concat_axis=0, tiled=True)
    valid = jnp.stack([slab + 1 < height, group > 0]).astype(jnp.int32)
    return upsample(
        valid, mixed, earlier, second, count, vectors, member, middle, up_weight
    )


def solution(mesh):
    placed = P("frames", "height", None, None)
    return jax.shard_map(
        local,
        mesh=mesh,
        in_specs=(placed,) + (P(),) * 11,
        out_specs=placed,
        check_vma=False,
    )
```
